256 devices in a mesh: row: 8 (over z_lo, core), col: 32 (over y, z_hi, x).
Axes of the slice: x: 4, y: 4, z: 8 (z_hi: 2, z_lo: 4; z = z_hi * 4 + z_lo), core: 2. Of those that a mesh axis runs over, the one named last changes fastest.
Arguments:
- spectra: bfloat16 [4, 1024, 8192], P(None, 'col', 'row'), may hold values from -6 to 6
- valid: int32 [1024, 8192], P('col', 'row'), may hold values 0 or 1
Outputs:
- cross: float32 [2, 2, 8192, 8192], P(None, None, 'row', 'col')
The draws below stay inside these ranges and needn't reach their ends.
All inputs are finite; a program needn't handle non-finite values. No bound on the sum of `valid` on one device may be relied on, other than what follows from the above.
Results may differ from the reference program's by a relative error of at most 0.003.
Values may be sent and summed in bfloat16 or wider, within the bound.
A program may use at most 128 MiB of HBM per device.

```python
import jax
import jax.numpy as jnp

NCH = 8192
FREQS = 2
WINDOWS = 1024


def place_ends(array, rng, low, top_value):
    index_at = [jax.random.randint(jax.random.fold_in(rng, axis), (), 0, length) for axis, length in enumerate(array.shape)]
    widest = array.shape.index(max(array.shape))
    beside = index_at[:widest] + [(index_at[widest] + 1) % array.shape[widest]] + index_at[widest + 1:]
    return array.at[tuple(index_at)].set(low).at[tuple(beside)].set(top_value)


def levels(own_key, extent, shards, smallest, largest):
    level = 1.0
    for position, blocks in shards:
        heights = jax.random.uniform(jax.random.fold_in(jax.random.fold_in(own_key, 6), position), (blocks,), jnp.float32, smallest / len(shards), largest / len(shards))
        level = level * jnp.repeat(jnp.exp(heights), extent[position] // blocks).reshape((-1,) + (1,) * (len(extent) - 1 - position))
    return level


def scatter_about(own_key, shape, scale, most, pieces=(), kind=jnp.bfloat16):
    factor_of = levels(own_key, shape, pieces, -0.22, 0.18) if pieces else 1.0
    array = jax.random.normal(own_key, shape, jnp.float32) * scale * factor_of
    return jnp.minimum(jnp.maximum(array, -most), most).astype(kind)


def setup_inputs(seed: int = 0) -> dict:
    keys = jax.random.split(jax.random.key(seed), 3)
    spectra = scatter_about(keys[0], (2 * FREQS, WINDOWS, NCH), 1.0, 6.0, ((1, 32), (2, 8)))
    valid = place_ends((jax.random.randint(keys[1], (WINDOWS, NCH), 0, 4) < 3).astype(jnp.int32), jax.random.fold_in(keys[1], 1), 0, 1)
    return dict(spectra=spectra, valid=valid)


def whiten(spectra, valid):
    values = spectra.astype(jnp.float32)
    real_part = values[0::2]
    imag_part = values[1::2]
    amplitude = jnp.sqrt(real_part * real_part + imag_part * imag_part)
    factor = valid.astype(jnp.float32)[None] / jnp.maximum(amplitude, 0.5)
    stacked = jnp.stack([real_part * factor, imag_part * factor], axis=1)
    return stacked.reshape(values.shape).astype(jnp.bfloat16)

def pair_dot(left, right):
    return jnp.dot(left.T, right, preferred_element_type=jnp.float32)

def reference(spectra, valid):
    white = whiten(spectra, valid)
    norm = 1.0 / jnp.sqrt(jnp.float32(WINDOWS))
    real_out = []
    imag_out = []
    for freq in range(FREQS):
        real_rows = white[2 * freq]
        imag_rows = white[2 * freq + 1]
        real_out.append((pair_dot(real_rows, real_rows) + pair_dot(imag_rows, imag_rows)) * norm)
        imag_out.append((pair_dot(imag_rows, real_rows) - pair_dot(real_rows, imag_rows)) * norm)
    return jnp.stack([jnp.stack(real_out), jnp.stack(imag_out)])
```

```python
import functools

import jax
import jax.numpy as jnp
from jax import lax
from jax.experimental import pallas as pl
from jax.experimental.pallas import tpu as pltpu
from jax.sharding import PartitionSpec as P

MESH = pl.DeviceIdType.MESH
RING = 4
LINE = 8


def device(x, y, z, core):
    return (lax.rem(z, 4) * 2 + core, y * 8 + lax.div(z, 4) * 4 + x)


def up(a, d, n):
    return lax.rem(a + (d + n), n)


def kernel(norm, spectra, valid, out, gathered, partner, z_send, z_recv, in_send, in_recv,
           out_send, out_recv, b_send, b_pass, b_side, b_recv):
    row = lax.axis_index("row")
    col = lax.axis_index("col")
    core = lax.rem(row, 2)
    low = lax.div(row, 2)
    x = lax.rem(col, 4)
    half = lax.rem(lax.div(col, 4), 2)
    y = lax.div(col, 8)
    z = half * 4 + low
    width = partner.shape[-1]
    windows = spectra.shape[1]
    lanes = pl.ds(pl.multiple_of(x * width, width), width)
    place = ((x, y), (y, x))

    def ring_device(f, inner, step):
        if (f == 0) == inner:
            return device(up(x, step, RING), y, z, core)
        return device(x, up(y, step, RING), z, core)

    sibling = device(x, y, z, 1 - core)

    barrier = pltpu.get_barrier_semaphore()
    greeted = [ring_device(0, inner, step) for inner in (True, False) for step in (1, -1)]
    greeted += [device(x, y, up(z, d, LINE), c) for d in range(1, LINE) for c in range(2)]
    greeted.append(sibling)
    for other in greeted:
        pl.semaphore_signal(barrier, inc=1, device_id=other, device_id_type=MESH)

    for f in range(2):
        real = spectra[2 * f].astype(jnp.float32)
        imag = spectra[2 * f + 1].astype(jnp.float32)
        amplitude = jnp.sqrt(real * real + imag * imag)
        factor = valid[...].astype(jnp.float32) / jnp.maximum(amplitude, 0.5)
        inner, outer = place[f]
        gathered[f, half, outer, inner, 0] = (real * factor).astype(jnp.bfloat16)
        gathered[f, half, outer, inner, 1] = (imag * factor).astype(jnp.bfloat16)
    pl.semaphore_wait(barrier, len(greeted))

    pending = []

    def send(ref, send_sem, recv_sem, target, landing=None, when=None):
        copy = pltpu.make_async_remote_copy(
            src_ref=ref,
            dst_ref=ref if landing is None else landing,
            send_sem=send_sem,
            recv_sem=recv_sem,
            device_id=target,
            device_id_type=MESH,
        )
        if when is None:
            copy.start()
        else:
            pl.when(when)(copy.start)
        pending.append((copy, when))

    def arrived(ref, recv_sem):
        pltpu.make_async_remote_copy(
            src_ref=ref,
            dst_ref=ref,
            send_sem=z_send.at[0],
            recv_sem=recv_sem,
            device_id=sibling,
            device_id_type=MESH,
        ).wait_recv()

    def side(r):
        return half if r == 0 else 1 - half

    inner_steps = (0, -1, 1, 2)

    def slot(f, r, do, di):
        inner, outer = place[f]
        return gathered.at[f, side(r), up(outer, do, RING), up(inner, di, RING)]

    def outer_send(f, r, j):
        block = slot(f, r, 0, inner_steps[j])
        for k, step in enumerate((1, -1)):
            send(block, out_send.at[r, f, k, j], out_recv.at[r, f, k, j], ring_device(f, False, step))

    def inner_start(f, r):
        block = slot(f, r, 0, 0)
        for k, step in enumerate((1, -1)):
            send(block, in_send.at[r, f, k], in_recv.at[r, f, k], ring_device(f, True, step))

    def inner_forward(f, r):
        for k, step in enumerate((1, -1)):
            block = slot(f, r, 0, -step)
            arrived(block, in_recv.at[r, f, k])
            send(block.at[k], in_send.at[r, f, 2 + k], in_recv.at[r, f, 2 + k], ring_device(f, True, step))
            outer_send(f, r, 1 + k)

    def inner_finish(f, r):
        block = slot(f, r, 0, 2)
        for k in range(2):
            arrived(block.at[k], in_recv.at[r, f, 2 + k])
        outer_send(f, r, 3)

    def outer_forward(f, r, j):
        for k, step in enumerate((1, -1)):
            block = slot(f, r, -step, inner_steps[j])
            arrived(block, out_recv.at[r, f, k, j])
            send(block.at[k], out_send.at[r, f, 2 + k, j], out_recv.at[r, f, 2 + k, j], ring_device(f, False, step))

    def outer_finish(f, r):
        for j in range(4):
            block = slot(f, r, 2, inner_steps[j])
            for k in range(2):
                arrived(block.at[k], out_recv.at[r, f, 2 + k, j])

    diagonal = low == y
    owner = jnp.logical_and(diagonal, core == half)
    outer_steps = (0, -1, 1, 2)

    def half_of(d):
        return lax.div(up(z, d, LINE), 4)

    def b_slot(f, h, rel):
        return partner.at[f, h, up(place[f][1], outer_steps[rel], RING)]

    def b_source(f, r, rel):
        return gathered.at[f, side(r), up(place[f][1], outer_steps[rel], RING), :, :, :, lanes]

    def b_start(f, rel):
        for k, step in enumerate((1, -1)):
            first = half_of(step) == core
            second = half_of(2 * step) == core
            third = half_of(3 * step) == core
            distance = jnp.where(first, 1, jnp.where(second, 2, 3))
            found = jnp.logical_or(first, jnp.logical_or(second, third))
            target = device(x, y, lax.rem(z + distance * step + LINE, LINE), f)
            send(b_source(f, 0, rel), b_send.at[k, f, rel], b_recv.at[half_index(0), f, rel], target,
                 landing=b_slot(f, half, rel), when=jnp.logical_and(diagonal, found))

    def half_index(r):
        return side(r)

    def b_local(f, r, rel):
        copy = pltpu.make_async_copy(b_source(f, r, rel), b_slot(f, side(r), rel), b_recv.at[side(r), f, rel])
        pl.when(owner)(copy.start)
        send(b_source(f, r, rel), b_side.at[r, f, rel], b_recv.at[side(r), f, rel], sibling,
             landing=b_slot(f, side(r), rel), when=owner)

    def b_wait(f, r, rel):
        block = b_slot(f, side(r), rel)
        arrived(block, b_recv.at[side(r), f, rel])

    def b_relay(f, r, rel):
        h = side(r)
        block = b_slot(f, h, rel)

        @pl.when(jnp.logical_not(diagonal))
        def _():
            b_wait(f, r, rel)

        mine = jnp.logical_and(jnp.logical_not(diagonal), core == f)
        send(block, b_side.at[r, f, rel], b_recv.at[h, f, rel], sibling, when=mine)
        distance = lax.rem(z - (y + 4 * h) + 2 * LINE, LINE)
        step = jnp.where(distance < 4, 1, -1)
        following = lax.rem(z + step + LINE, LINE)
        goes_on = jnp.logical_and(
            jnp.logical_and(distance != 3, distance != 5), lax.div(following, 4) == half
        )
        send(block, b_pass.at[r, f, rel], b_recv.at[h, f, rel], device(x, y, following, core),
             when=jnp.logical_and(mine, goes_on))

    def chunk(f, r, rel, first=False, last=False):
        h = side(r)
        outer = up(place[f][1], outer_steps[rel], RING)
        depth = RING * 2 * windows
        block = partner[f, h, outer]
        turned = jnp.stack([-block[:, 1], block[:, 0]], axis=1)
        right = jnp.concatenate([block.reshape(depth, width), turned.reshape(depth, width)], axis=1)
        tile = 256

        @pl.loop(0, gathered.shape[-1] // tile)
        def _(t):
            rows = pl.ds(pl.multiple_of(t * tile, tile), tile)
            left = gathered[f, h, outer, :, :, :, rows].reshape(depth, tile)
            product = lax.dot_general(
                left, right, (((0,), (0,)), ((), ())), preferred_element_type=jnp.float32
            )
            for p in range(2):
                part = product[:, p * width:(p + 1) * width]
                if not first:
                    part = out[p, f, rows, :] + part
                if last:
                    part = part * norm
                out[p, f, rows, :] = part

    both = range(2)
    for f in both:
        send(slot(f, 0, 0, 0), z_send.at[f], z_recv.at[f], device(x, y, up(z, 4, LINE), core))
        inner_start(f, 0)
    for f in both:
        outer_send(f, 0, 0)
    for f in both:
        inner_forward(f, 0)
    for f in both:
        inner_finish(f, 0)
        b_start(f, 0)
        b_local(f, 0, 0)
    for f in both:
        outer_forward(f, 0, 0)
    for f in both:
        outer_forward(f, 0, 1)
    for f in both:
        arrived(slot(f, 1, 0, 0), z_recv.at[f])
        inner_start(f, 1)
        outer_send(f, 1, 0)
    for f in both:
        outer_forward(f, 0, 2)
    for f in both:
        for r in range(2):
            b_relay(f, r, 0)
    for f in both:
        outer_forward(f, 0, 3)
        for rel in (1, 2):
            b_start(f, rel)
            b_local(f, 0, rel)
    for f in both:
        inner_forward(f, 1)
    for f in both:
        outer_finish(f, 0)
        b_start(f, 3)
        b_local(f, 0, 3)
    for f in both:
        inner_finish(f, 1)
        b_local(f, 1, 0)

    def own_wait(f, r, rel):
        pl.when(diagonal)(functools.partial(b_wait, f, r, rel))

    for f in both:
        outer_forward(f, 1, 0)
        own_wait(f, 0, 0)
        chunk(f, 0, 0, first=True)
    for rel in (1, 2):
        for f in both:
            for r in range(2):
                b_relay(f, r, rel)
            outer_forward(f, 1, rel)
            own_wait(f, 0, rel)
            chunk(f, 0, rel)
    for f in both:
        for r in range(2):
            b_relay(f, r, 3)
        outer_forward(f, 1, 3)
    for f in both:
        for rel in (1, 2):
            b_local(f, 1, rel)
        own_wait(f, 0, 3)
        chunk(f, 0, 3)
    for rel in (0, 1, 2):
        for f in both:
            own_wait(f, 1, rel)
            chunk(f, 1, rel)
    for f in both:
        outer_finish(f, 1)
        b_local(f, 1, 3)
        own_wait(f, 1, 3)
        chunk(f, 1, 3, last=True)

    for copy, when in pending:
        if when is None:
            copy.wait_send()
        else:
            pl.when(when)(copy.wait_send)


def on_device(spectra, valid):
    planes, windows, rows = spectra.shape
    width = rows // 4
    total = windows * lax.axis_size("col")
    norm = 1.0 / float(total) ** 0.5
    dma = pltpu.SemaphoreType.DMA
    vmem = pl.BlockSpec(memory_space=pltpu.VMEM)
    return pl.pallas_call(
        functools.partial(kernel, norm),
        out_shape=jax.ShapeDtypeStruct((2, planes // 2, rows, width), jnp.float32),
        in_specs=[vmem, vmem],
        out_specs=vmem,
        scratch_shapes=[
            pltpu.VMEM((2, 2, RING, RING, 2, windows, rows), jnp.bfloat16),
            pltpu.VMEM((2, 2, RING, RING, 2, windows, width), jnp.bfloat16),
            dma((2,)),
            dma((2,)),
            dma((2, 2, 4)),
            dma((2, 2, 4)),
            dma((2, 2, 4, 4)),
            dma((2, 2, 4, 4)),
            dma((2, 2, 4)),
            dma((2, 2, 4)),
            dma((2, 2, 4)),
            dma((2, 2, 4)),
        ],
        compiler_params=pltpu.CompilerParams(
            collective_id=0, has_side_effects=True, vmem_limit_bytes=48 * 2**20
        ),
        cost_estimate=pl.CostEstimate(
            flops=16 * total * rows * width, bytes_accessed=2**22, transcendentals=0
        ),
    )(spectra, valid)


def solution(mesh):
    placed = (P(None, "col", "row"), P("col", "row"))
    return jax.shard_map(
        on_device,
        mesh=mesh,
        in_specs=placed,
        out_specs=P(None, None, "row", "col"),
        check_vma=False,
    )
```

```python
import functools

import jax
import jax.numpy as jnp
from jax import lax
from jax.experimental import pallas as pl
from jax.experimental.pallas import tpu as pltpu
from jax.sharding import PartitionSpec as P

MESH = pl.DeviceIdType.MESH
RING = 4
LINE = 8


def device(x, y, z, core):
    return (lax.rem(z, 4) * 2 + core, y * 8 + lax.div(z, 4) * 4 + x)


def up(a, d, n):
    return lax.rem(a + (d + n), n)


def kernel(norm, spectra, valid, out, gathered, partner, z_send, z_recv, in_send, in_recv,
           out_send, out_recv, b_send, b_pass, b_far, b_side, b_recv):
    row = lax.axis_index("row")
    col = lax.axis_index("col")
    core = lax.rem(row, 2)
    low = lax.div(row, 2)
    x = lax.rem(col, 4)
    half = lax.rem(lax.div(col, 4), 2)
    y = lax.div(col, 8)
    z = half * 4 + low
    width = partner.shape[-1]
    windows = spectra.shape[1]
    lanes = pl.ds(pl.multiple_of(x * width, width), width)
    place = ((x, y), (y, x))

    def ring_device(f, inner, step):
        if (f == 0) == inner:
            return device(up(x, step, RING), y, z, core)
        return device(x, up(y, step, RING), z, core)

    sibling = device(x, y, z, 1 - core)

    barrier = pltpu.get_barrier_semaphore()
    greeted = [ring_device(0, inner, step) for inner in (True, False) for step in (1, -1)]
    greeted += [device(x, y, up(z, d, LINE), c) for d in range(1, LINE) for c in range(2)]
    greeted.append(sibling)
    for other in greeted:
        pl.semaphore_signal(barrier, inc=1, device_id=other, device_id_type=MESH)

    for f in range(2):
        real = spectra[2 * f].astype(jnp.float32)
        imag = spectra[2 * f + 1].astype(jnp.float32)
        amplitude = jnp.sqrt(real * real + imag * imag)
        factor = valid[...].astype(jnp.float32) / jnp.maximum(amplitude, 0.5)
        inner, outer = place[f]
        gathered[f, half, outer, inner, 0] = (real * factor).astype(jnp.bfloat16)
        gathered[f, half, outer, inner, 1] = (imag * factor).astype(jnp.bfloat16)
    pl.semaphore_wait(barrier, len(greeted))

    pending = []

    def send(ref, send_sem, recv_sem, target, landing=None, when=None):
        copy = pltpu.make_async_remote_copy(
            src_ref=ref,
            dst_ref=ref if landing is None else landing,
            send_sem=send_sem,
            recv_sem=recv_sem,
            device_id=target,
            device_id_type=MESH,
        )
        if when is None:
            copy.start()
        else:
            pl.when(when)(copy.start)
        pending.append((copy, when))

    def arrived(ref, recv_sem):
        pltpu.make_async_remote_copy(
            src_ref=ref,
            dst_ref=ref,
            send_sem=z_send.at[0],
            recv_sem=recv_sem,
            device_id=sibling,
            device_id_type=MESH,
        ).wait_recv()

    def side(r):
        return half if r == 0 else 1 - half

    inner_steps = (0, -1, 1, 2)

    def slot(f, r, do, di):
        inner, outer = place[f]
        return gathered.at[f, side(r), up(outer, do, RING), up(inner, di, RING)]

    def outer_send(f, r, j):
        block = slot(f, r, 0, inner_steps[j])
        for k, step in enumerate((1, -1)):
            send(block, out_send.at[r, f, k, j], out_recv.at[r, f, k, j], ring_device(f, False, step))

    def inner_start(f, r):
        block = slot(f, r, 0, 0)
        for k, step in enumerate((1, -1)):
            send(block, in_send.at[r, f, k], in_recv.at[r, f, k], ring_device(f, True, step))

    def inner_forward(f, r):
        for k, step in enumerate((1, -1)):
            block = slot(f, r, 0, -step)
            arrived(block, in_recv.at[r, f, k])
            send(block.at[k], in_send.at[r, f, 2 + k], in_recv.at[r, f, 2 + k], ring_device(f, True, step))
            outer_send(f, r, 1 + k)

    def inner_finish(f, r):
        block = slot(f, r, 0, 2)
        for k in range(2):
            arrived(block.at[k], in_recv.at[r, f, 2 + k])
        outer_send(f, r, 3)

    def outer_forward(f, r, j):
        for k, step in enumerate((1, -1)):
            block = slot(f, r, -step, inner_steps[j])
            arrived(block, out_recv.at[r, f, k, j])
            send(block.at[k], out_send.at[r, f, 2 + k, j], out_recv.at[r, f, 2 + k, j], ring_device(f, False, step))

    def outer_finish(f, r):
        for j in range(4):
            block = slot(f, r, 2, inner_steps[j])
            for k in range(2):
                arrived(block.at[k], out_recv.at[r, f, 2 + k, j])

    diagonal = low == y
    owner = jnp.logical_and(diagonal, core == half)
    outer_steps = (0, -1, 1, 2)

    def half_of(d):
        return lax.div(up(z, d, LINE), 4)

    def b_slot(f, h, rel):
        return partner.at[f, h, up(place[f][1], outer_steps[rel], RING)]

    def b_source(f, r, rel):
        return gathered.at[f, side(r), up(place[f][1], outer_steps[rel], RING), :, :, :, lanes]

    def b_start(f, rel):
        for k, step in enumerate((1, -1)):
            fits = [half_of(d * step) == core for d in (1, 2, 3)]
            nearest = jnp.where(fits[0], 1, jnp.where(fits[1], 2, 3))
            found = jnp.logical_or(fits[0], jnp.logical_or(fits[1], fits[2]))
            third = jnp.logical_and(fits[0], fits[2])
            for n, (distance, when) in enumerate(((nearest, found), (3, third))):
                target = device(x, y, lax.rem(z + distance * step + LINE, LINE), f)
                send(b_source(f, 0, rel), b_send.at[k, n, f, rel], b_recv.at[half, f, rel], target,
                     landing=b_slot(f, half, rel), when=jnp.logical_and(diagonal, when))

    def b_local(f, r, rel):
        copy = pltpu.make_async_copy(b_source(f, r, rel), b_slot(f, side(r), rel), b_recv.at[side(r), f, rel])
        pl.when(owner)(copy.start)
        send(b_source(f, r, rel), b_side.at[r, f, rel], b_recv.at[side(r), f, rel], sibling,
             landing=b_slot(f, side(r), rel), when=owner)

    def b_wait(f, r, rel):
        arrived(b_slot(f, side(r), rel), b_recv.at[side(r), f, rel])

    def b_place(r):
        distance = lax.rem(z - (y + 4 * side(r)) + 2 * LINE, LINE)
        step = jnp.where(distance < 4, 1, -1)
        steps = jnp.where(distance < 4, distance, LINE - distance)
        before = lax.rem(z - step + LINE, LINE)
        after = lax.rem(z + step + LINE, LINE)
        nearest = jnp.logical_or(steps == 1, lax.div(before, 4) != half)
        goes_on = jnp.logical_and(nearest, jnp.logical_and(steps != 3, lax.div(after, 4) == half))
        return nearest, goes_on, after

    def b_pass_on(f, r, rel, nearest):
        h = side(r)
        block = b_slot(f, h, rel)
        is_nearest, goes_on, after = b_place(r)
        mine = jnp.logical_and(jnp.logical_not(diagonal), core == f)
        mine = jnp.logical_and(mine, is_nearest if nearest else jnp.logical_not(is_nearest))
        pl.when(mine)(functools.partial(b_wait, f, r, rel))
        if nearest:
            send(block, b_pass.at[r, f, rel], b_recv.at[h, f, rel], device(x, y, after, core),
                 when=jnp.logical_and(mine, goes_on))
        send(block, b_far.at[int(nearest), r, f, rel], b_recv.at[h, f, rel], sibling, when=mine)

    def b_need(f, r, rel):
        pl.when(jnp.logical_or(diagonal, core != f))(functools.partial(b_wait, f, r, rel))

    def chunk(f, r, rel, first=False, last=False):
        h = side(r)
        outer = up(place[f][1], outer_steps[rel], RING)
        depth = RING * 2 * windows
        block = partner[f, h, outer]
        turned = jnp.stack([-block[:, 1], block[:, 0]], axis=1)
        right = jnp.concatenate([block.reshape(depth, width), turned.reshape(depth, width)], axis=1)
        tile = 256

        @pl.loop(0, gathered.shape[-1] // tile)
        def _(t):
            rows = pl.ds(pl.multiple_of(t * tile, tile), tile)
            left = gathered[f, h, outer, :, :, :, rows].reshape(depth, tile)
            product = lax.dot_general(
                left, right, (((0,), (0,)), ((), ())), preferred_element_type=jnp.float32
            )
            for p in range(2):
                part = product[:, p * width:(p + 1) * width]
                if not first:
                    part = out[p, f, rows, :] + part
                if last:
                    part = part * norm
                out[p, f, rows, :] = part

    both = range(2)

    def b_nearest(*rels):
        for rel in rels:
            for f in both:
                for r in both:
                    b_pass_on(f, r, rel, True)

    def b_rest(*rels):
        for rel in rels:
            for f in both:
                for r in both:
                    b_pass_on(f, r, rel, False)

    def forward(r, j):
        for f in both:
            outer_forward(f, r, j)

    def work(r, rel, **ends):
        for f in both:
            b_need(f, r, rel)
            chunk(f, r, rel, **ends)

    for f in both:
        send(slot(f, 0, 0, 0), z_send.at[f], z_recv.at[f], device(x, y, up(z, 4, LINE), core))
        inner_start(f, 0)
    for f in both:
        outer_send(f, 0, 0)
    for f in both:
        inner_forward(f, 0)
    for f in both:
        inner_finish(f, 0)
        b_start(f, 0)
        b_local(f, 0, 0)
    forward(0, 0)
    forward(0, 1)
    for f in both:
        arrived(slot(f, 1, 0, 0), z_recv.at[f])
        inner_start(f, 1)
        outer_send(f, 1, 0)
    forward(0, 2)
    b_nearest(0)
    forward(0, 3)
    for f in both:
        for rel in (1, 2):
            b_start(f, rel)
            b_local(f, 0, rel)
    for f in both:
        inner_forward(f, 1)
    for f in both:
        outer_finish(f, 0)
        b_start(f, 3)
        b_local(f, 0, 3)
    b_rest(0)
    for f in both:
        inner_finish(f, 1)
        b_local(f, 1, 0)
    forward(1, 0)
    work(0, 0, first=True)
    b_nearest(1, 2)
    work(1, 0)
    forward(1, 1)
    b_rest(1, 2)
    b_nearest(3)
    forward(1, 2)
    work(0, 1)
    b_rest(3)
    work(0, 2)
    forward(1, 3)
    for f in both:
        for rel in (1, 2):
            b_local(f, 1, rel)
    work(0, 3)
    work(1, 1)
    work(1, 2)
    for f in both:
        outer_finish(f, 1)
        b_local(f, 1, 3)
        b_need(f, 1, 3)
        chunk(f, 1, 3, last=True)

    for copy, when in pending:
        if when is None:
            copy.wait_send()
        else:
            pl.when(when)(copy.wait_send)


def on_device(spectra, valid):
    planes, windows, rows = spectra.shape
    width = rows // 4
    total = windows * lax.axis_size("col")
    norm = 1.0 / float(total) ** 0.5
    dma = pltpu.SemaphoreType.DMA
    vmem = pl.BlockSpec(memory_space=pltpu.VMEM)
    return pl.pallas_call(
        functools.partial(kernel, norm),
        out_shape=jax.ShapeDtypeStruct((2, planes // 2, rows, width), jnp.float32),
        in_specs=[vmem, vmem],
        out_specs=vmem,
        scratch_shapes=[
            pltpu.VMEM((2, 2, RING, RING, 2, windows, rows), jnp.bfloat16),
            pltpu.VMEM((2, 2, RING, RING, 2, windows, width), jnp.bfloat16),
            dma((2,)),
            dma((2,)),
            dma((2, 2, 4)),
            dma((2, 2, 4)),
            dma((2, 2, 4, 4)),
            dma((2, 2, 4, 4)),
            dma((2, 2, 2, 4)),
            dma((2, 2, 4)),
            dma((2, 2, 2, 4)),
            dma((2, 2, 4)),
            dma((2, 2, 4)),
        ],
        compiler_params=pltpu.CompilerParams(
            collective_id=0, has_side_effects=True, vmem_limit_bytes=48 * 2**20
        ),
        cost_estimate=pl.CostEstimate(
            flops=16 * total * rows * width, bytes_accessed=2**22, transcendentals=0
        ),
    )(spectra, valid)


def solution(mesh):
    placed = (P(None, "col", "row"), P("col", "row"))
    return jax.shard_map(
        on_device,
        mesh=mesh,
        in_specs=placed,
        out_specs=P(None, None, "row", "col"),
        check_vma=False,
    )
```

```python
import functools

import jax
import jax.numpy as jnp
from jax import lax
from jax.experimental import pallas as pl
from jax.experimental.pallas import tpu as pltpu
from jax.sharding import PartitionSpec as P

MESH = pl.DeviceIdType.MESH
RING = 4
LINE = 8


def device(x, y, z, core):
    return (lax.rem(z, 4) * 2 + core, y * 8 + lax.div(z, 4) * 4 + x)


def up(a, d, n):
    return lax.rem(a + (d + n), n)


def kernel(norm, spectra, valid, out, gathered, partner, z_send, z_recv, in_send, in_recv,
           out_send, out_recv, b_send, b_pass, b_far, b_side, b_recv):
    row = lax.axis_index("row")
    col = lax.axis_index("col")
    core = lax.rem(row, 2)
    low = lax.div(row, 2)
    x = lax.rem(col, 4)
    half = lax.rem(lax.div(col, 4), 2)
    y = lax.div(col, 8)
    z = half * 4 + low
    width = partner.shape[-1]
    windows = spectra.shape[1]
    lanes = pl.ds(pl.multiple_of(x * width, width), width)
    place = ((x, y), (y, x))

    def ring_device(f, inner, step):
        if (f == 0) == inner:
            return device(up(x, step, RING), y, z, core)
        return device(x, up(y, step, RING), z, core)

    sibling = device(x, y, z, 1 - core)

    barrier = pltpu.get_barrier_semaphore()
    greeted = [ring_device(0, inner, step) for inner in (True, False) for step in (1, -1)]
    greeted += [device(x, y, up(z, d, LINE), c) for d in range(1, LINE) for c in range(2)]
    greeted.append(sibling)
    for other in greeted:
        pl.semaphore_signal(barrier, inc=1, device_id=other, device_id_type=MESH)

    for f in range(2):
        real = spectra[2 * f].astype(jnp.float32)
        imag = spectra[2 * f + 1].astype(jnp.float32)
        amplitude = jnp.sqrt(real * real + imag * imag)
        factor = valid[...].astype(jnp.float32) / jnp.maximum(amplitude, 0.5)
        inner, outer = place[f]
        gathered[f, half, outer, inner, 0] = (real * factor).astype(jnp.bfloat16)
        gathered[f, half, outer, inner, 1] = (imag * factor).astype(jnp.bfloat16)
    pl.semaphore_wait(barrier, len(greeted))

    pending = []

    def send(ref, send_sem, recv_sem, target, landing=None, when=None):
        copy = pltpu.make_async_remote_copy(
            src_ref=ref,
            dst_ref=ref if landing is None else landing,
            send_sem=send_sem,
            recv_sem=recv_sem,
            device_id=target,
            device_id_type=MESH,
        )
        if when is None:
            copy.start()
        else:
            pl.when(when)(copy.start)
        pending.append((copy, when))

    def arrived(ref, recv_sem):
        pltpu.make_async_remote_copy(
            src_ref=ref,
            dst_ref=ref,
            send_sem=z_send.at[0],
            recv_sem=recv_sem,
            device_id=sibling,
            device_id_type=MESH,
        ).wait_recv()

    def side(r):
        return half if r == 0 else 1 - half

    inner_steps = (0, -1, 1, 2)

    def slot(f, r, do, di):
        inner, outer = place[f]
        return gathered.at[f, side(r), up(outer, do, RING), up(inner, di, RING)]

    def plane_order(k):
        return (k, 1 - k)

    def outer_plane(f, r, j, k, p):
        send(slot(f, r, 0, inner_steps[j]).at[p], out_send.at[r, f, k, j, p], out_recv.at[r, f, k, j, p],
             ring_device(f, False, (1, -1)[k]))

    def outer_send(f, r, j):
        for n in range(2):
            for k in range(2):
                outer_plane(f, r, j, k, plane_order(k)[n])

    def inner_start(f, r):
        block = slot(f, r, 0, 0)
        for n in range(2):
            for k, step in enumerate((1, -1)):
                p = plane_order(k)[n]
                send(block.at[p], in_send.at[r, f, k, p], in_recv.at[r, f, k, p], ring_device(f, True, step))

    def inner_forward(f, r):
        for k, step in enumerate((1, -1)):
            plane = slot(f, r, 0, -step).at[k]
            arrived(plane, in_recv.at[r, f, k, k])
            send(plane, in_send.at[r, f, 2 + k, 0], in_recv.at[r, f, 2 + k, 0], ring_device(f, True, step))

    def inner_rest(f, r):
        for k, step in enumerate((1, -1)):
            arrived(slot(f, r, 0, -step).at[1 - k], in_recv.at[r, f, k, 1 - k])
            outer_send(f, r, 1 + k)

    def inner_finish(f, r):
        block = slot(f, r, 0, 2)
        for k in range(2):
            arrived(block.at[k], in_recv.at[r, f, 2 + k, 0])
        outer_send(f, r, 3)

    def outer_forward(f, r, j):
        for k, step in enumerate((1, -1)):
            plane = slot(f, r, -step, inner_steps[j]).at[k]
            arrived(plane, out_recv.at[r, f, k, j, k])
            send(plane, out_send.at[r, f, 2 + k, j, 0], out_recv.at[r, f, 2 + k, j, 0], ring_device(f, False, step))

    def outer_rest(f, r, j):
        for k, step in enumerate((1, -1)):
            arrived(slot(f, r, -step, inner_steps[j]).at[1 - k], out_recv.at[r, f, k, j, 1 - k])

    def outer_finish(f, r, j):
        block = slot(f, r, 2, inner_steps[j])
        for k in range(2):
            arrived(block.at[k], out_recv.at[r, f, 2 + k, j, 0])

    diagonal = low == y
    owner = jnp.logical_and(diagonal, core == half)
    outer_steps = (0, -1, 1, 2)

    def half_of(d):
        return lax.div(up(z, d, LINE), 4)

    def b_slot(f, h, rel):
        return partner.at[f, h, up(place[f][1], outer_steps[rel], RING)]

    def b_start(f, rel, j):
        inner, outer = place[f]
        outer = up(outer, outer_steps[rel], RING)
        inner = up(inner, inner_steps[j], RING)
        piece = gathered.at[f, half, outer, inner, :, :, lanes]
        landing = partner.at[f, half, outer, inner]
        for k, step in enumerate((1, -1)):
            fits = [half_of(d * step) == core for d in (1, 2, 3)]
            nearest = jnp.where(fits[0], 1, jnp.where(fits[1], 2, 3))
            found = jnp.logical_or(fits[0], jnp.logical_or(fits[1], fits[2]))
            third = jnp.logical_and(fits[0], fits[2])
            for n, (distance, when) in enumerate(((nearest, found), (3, third))):
                target = device(x, y, lax.rem(z + distance * step + LINE, LINE), f)
                send(piece, b_send.at[k, n, f, rel, j], b_recv.at[half, f, rel], target,
                     landing=landing, when=jnp.logical_and(diagonal, when))

    def b_local(f, r, rel, j):
        inner, outer = place[f]
        outer = up(outer, outer_steps[rel], RING)
        inner = up(inner, inner_steps[j], RING)

        @pl.when(owner)
        def _():
            partner[f, side(r), outer, inner] = gathered[f, side(r), outer, inner, :, :, lanes]

        send(gathered.at[f, side(r), outer, inner, :, :, lanes], b_side.at[r, f, rel, j],
             b_recv.at[side(r), f, rel], sibling, landing=partner.at[f, side(r), outer, inner], when=owner)

    def b_wait(f, r, rel):
        arrived(b_slot(f, side(r), rel), b_recv.at[side(r), f, rel])

    def b_place(r):
        distance = lax.rem(z - (y + 4 * side(r)) + 2 * LINE, LINE)
        step = jnp.where(distance < 4, 1, -1)
        steps = jnp.where(distance < 4, distance, LINE - distance)
        before = lax.rem(z - step + LINE, LINE)
        after = lax.rem(z + step + LINE, LINE)
        nearest = jnp.logical_or(steps == 1, lax.div(before, 4) != half)
        goes_on = jnp.logical_and(nearest, jnp.logical_and(steps != 3, lax.div(after, 4) == half))
        return nearest, goes_on, after

    def b_pass_on(f, r, rel, nearest):
        h = side(r)
        block = b_slot(f, h, rel)
        is_nearest, goes_on, after = b_place(r)
        mine = jnp.logical_and(jnp.logical_not(diagonal), core == f)
        mine = jnp.logical_and(mine, is_nearest if nearest else jnp.logical_not(is_nearest))
        pl.when(mine)(functools.partial(b_wait, f, r, rel))
        if nearest:
            send(block, b_pass.at[r, f, rel], b_recv.at[h, f, rel], device(x, y, after, core),
                 when=jnp.logical_and(mine, goes_on))
        send(block, b_far.at[int(nearest), r, f, rel], b_recv.at[h, f, rel], sibling, when=mine)

    def b_need(f, r, rel):
        needed = jnp.logical_or(jnp.logical_and(diagonal, core != half), jnp.logical_and(jnp.logical_not(diagonal), core != f))
        pl.when(needed)(functools.partial(b_wait, f, r, rel))

    def chunk(f, r, rel, first=False, last=False):
        h = side(r)
        outer = up(place[f][1], outer_steps[rel], RING)
        depth = RING * 2 * windows
        block = partner[f, h, outer]
        turned = jnp.stack([-block[:, 1], block[:, 0]], axis=1)
        right = jnp.concatenate([block.reshape(depth, width), turned.reshape(depth, width)], axis=1)
        left = gathered[f, h, outer].reshape(depth, gathered.shape[-1])
        product = lax.dot_general(
            left, right, (((0,), (0,)), ((), ())), preferred_element_type=jnp.float32
        )
        for p in range(2):
            part = product[:, p * width:(p + 1) * width]
            if not first:
                part = out[p, f] + part
            if last:
                part = part * norm
            out[p, f] = part

    both = range(2)

    def b_nearest(*rels):
        for rel in rels:
            for f in both:
                for r in both:
                    b_pass_on(f, r, rel, True)

    def b_rest(*rels):
        for rel in rels:
            for f in both:
                for r in both:
                    b_pass_on(f, r, rel, False)

    def work(r, rel, **ends):
        for f in both:
            b_need(f, r, rel)
            chunk(f, r, rel, **ends)

    for f in both:
        send(slot(f, 0, 0, 0), z_send.at[f], z_recv.at[f], device(x, y, up(z, 4, LINE), core))
    for f in both:
        inner_start(f, 0)
    for f in both:
        outer_send(f, 0, 0)
    for f in both:
        inner_forward(f, 0)
    for f in both:
        inner_rest(f, 0)
    for f in both:
        inner_finish(f, 0)
        b_start(f, 0, 0)
        b_local(f, 0, 0, 0)
        b_start(f, 0, 1)
        b_local(f, 0, 0, 1)
        b_start(f, 0, 2)
        b_local(f, 0, 0, 2)
        b_start(f, 0, 3)
        b_local(f, 0, 0, 3)
    for f in both:
        outer_forward(f, 0, 0)
    for f in both:
        outer_rest(f, 0, 0)
        b_start(f, 1, 0)
        b_local(f, 0, 1, 0)
        b_start(f, 2, 0)
        b_local(f, 0, 2, 0)
    for f in both:
        outer_forward(f, 0, 1)
    for f in both:
        outer_rest(f, 0, 1)
        b_start(f, 1, 1)
        b_local(f, 0, 1, 1)
        b_start(f, 2, 1)
        b_local(f, 0, 2, 1)
    for f in both:
        arrived(slot(f, 1, 0, 0), z_recv.at[f])
        inner_start(f, 1)
        outer_send(f, 1, 0)
    for f in both:
        outer_forward(f, 0, 2)
    for f in both:
        outer_rest(f, 0, 2)
        b_start(f, 1, 2)
        b_local(f, 0, 1, 2)
        b_start(f, 2, 2)
        b_local(f, 0, 2, 2)
    b_nearest(0)
    for f in both:
        outer_forward(f, 0, 3)
    for f in both:
        outer_rest(f, 0, 3)
        b_start(f, 1, 3)
        b_local(f, 0, 1, 3)
        b_start(f, 2, 3)
        b_local(f, 0, 2, 3)
    for f in both:
        inner_forward(f, 1)
    for f in both:
        inner_rest(f, 1)
    for f in both:
        outer_finish(f, 0, 0)
        b_start(f, 3, 0)
        b_local(f, 0, 3, 0)
        outer_finish(f, 0, 1)
        b_start(f, 3, 1)
        b_local(f, 0, 3, 1)
        outer_finish(f, 0, 2)
        b_start(f, 3, 2)
        b_local(f, 0, 3, 2)
        outer_finish(f, 0, 3)
        b_start(f, 3, 3)
        b_local(f, 0, 3, 3)
    b_rest(0)
    for f in both:
        inner_finish(f, 1)
    for f in both:
        b_local(f, 1, 0, 0)
        b_local(f, 1, 0, 1)
        b_local(f, 1, 0, 2)
        b_local(f, 1, 0, 3)
    for f in both:
        outer_forward(f, 1, 0)
    for f in both:
        outer_forward(f, 1, 1)
    for f in both:
        outer_rest(f, 1, 0)
        b_local(f, 1, 1, 0)
        b_local(f, 1, 2, 0)
    b_nearest(1)
    b_nearest(2)
    work(0, 0, first=True)
    work(1, 0)
    for f in both:
        outer_forward(f, 1, 2)
    for f in both:
        outer_rest(f, 1, 1)
        b_local(f, 1, 1, 1)
        b_local(f, 1, 2, 1)
    b_rest(1)
    b_rest(2)
    b_nearest(3)
    for f in both:
        outer_forward(f, 1, 3)
    for f in both:
        outer_rest(f, 1, 2)
        b_local(f, 1, 1, 2)
        b_local(f, 1, 2, 2)
    for f in both:
        outer_rest(f, 1, 3)
        b_local(f, 1, 1, 3)
        b_local(f, 1, 2, 3)
    work(0, 1)
    b_rest(3)
    work(0, 2)
    work(0, 3)
    work(1, 1)
    work(1, 2)
    for f in both:
        outer_finish(f, 1, 0)
        b_local(f, 1, 3, 0)
        outer_finish(f, 1, 1)
        b_local(f, 1, 3, 1)
        outer_finish(f, 1, 2)
        b_local(f, 1, 3, 2)
        outer_finish(f, 1, 3)
        b_local(f, 1, 3, 3)
    work(1, 3, last=True)

    for copy, when in pending:
        if when is None:
            copy.wait_send()
        else:
            pl.when(when)(copy.wait_send)


def on_device(spectra, valid):
    planes, windows, rows = spectra.shape
    width = rows // 4
    total = windows * lax.axis_size("col")
    norm = 1.0 / float(total) ** 0.5
    dma = pltpu.SemaphoreType.DMA
    vmem = pl.BlockSpec(memory_space=pltpu.VMEM)
    return pl.pallas_call(
        functools.partial(kernel, norm),
        out_shape=jax.ShapeDtypeStruct((2, planes // 2, rows, width), jnp.float32),
        in_specs=[vmem, vmem],
        out_specs=vmem,
        scratch_shapes=[
            pltpu.VMEM((2, 2, RING, RING, 2, windows, rows), jnp.bfloat16),
            pltpu.VMEM((2, 2, RING, RING, 2, windows, width), jnp.bfloat16),
            dma((2,)),
            dma((2,)),
            dma((2, 2, 4, 2)),
            dma((2, 2, 4, 2)),
            dma((2, 2, 4, 4, 2)),
            dma((2, 2, 4, 4, 2)),
            dma((2, 2, 2, 4, 4)),
            dma((2, 2, 4)),
            dma((2, 2, 2, 4)),
            dma((2, 2, 4, 4)),
            dma((2, 2, 4)),
        ],
        compiler_params=pltpu.CompilerParams(
            collective_id=0, has_side_effects=True, vmem_limit_bytes=48 * 2**20
        ),
        cost_estimate=pl.CostEstimate(
            flops=16 * total * rows * width, bytes_accessed=2**22, transcendentals=0
        ),
    )(spectra, valid)


def solution(mesh):
    placed = (P(None, "col", "row"), P("col", "row"))
    return jax.shard_map(
        on_device,
        mesh=mesh,
        in_specs=placed,
        out_specs=P(None, None, "row", "col"),
        check_vma=False,
    )
```

```python
import functools

import jax
import jax.numpy as jnp
from jax import lax
from jax.experimental import pallas as pl
from jax.experimental.pallas import tpu as pltpu
from jax.sharding import PartitionSpec as P

MESH = pl.DeviceIdType.MESH
RING = 4
LINE = 8


def device(x, y, z, core):
    return (lax.rem(z, 4) * 2 + core, y * 8 + lax.div(z, 4) * 4 + x)


def up(a, d, n):
    return lax.rem(a + (d + n), n)


def kernel(norm, spectra, valid, out, gathered, partner, a_send, z_recv, in_recv, out_recv,
           b_send, b_pass, b_far, b_side, b_recv):
    row = lax.axis_index("row")
    col = lax.axis_index("col")
    core = lax.rem(row, 2)
    low = lax.div(row, 2)
    x = lax.rem(col, 4)
    half = lax.rem(lax.div(col, 4), 2)
    y = lax.div(col, 8)
    z = half * 4 + low
    width = partner.shape[-1]
    windows = spectra.shape[1]
    lanes = pl.ds(pl.multiple_of(x * width, width), width)
    place = ((x, y), (y, x))

    def ring_device(f, inner, step):
        if (f == 0) == inner:
            return device(up(x, step, RING), y, z, core)
        return device(x, up(y, step, RING), z, core)

    sibling = device(x, y, z, 1 - core)

    barrier = pltpu.get_barrier_semaphore()
    greeted = [ring_device(0, inner, step) for inner in (True, False) for step in (1, -1)]
    greeted += [device(x, y, up(z, d, LINE), c) for d in range(1, LINE) for c in range(2)]
    greeted.append(sibling)
    for other in greeted:
        pl.semaphore_signal(barrier, inc=1, device_id=other, device_id_type=MESH)

    for f in range(2):
        real = spectra[2 * f].astype(jnp.float32)
        imag = spectra[2 * f + 1].astype(jnp.float32)
        amplitude = jnp.sqrt(real * real + imag * imag)
        factor = valid[...].astype(jnp.float32) / jnp.maximum(amplitude, 0.5)
        inner, outer = place[f]
        gathered[f, half, outer, inner, 0] = (real * factor).astype(jnp.bfloat16)
        gathered[f, half, outer, inner, 1] = (imag * factor).astype(jnp.bfloat16)
    pl.semaphore_wait(barrier, len(greeted))

    def send(ref, send_sem, recv_sem, target, landing=None, when=None):
        copy = pltpu.make_async_remote_copy(
            src_ref=ref,
            dst_ref=ref if landing is None else landing,
            send_sem=send_sem,
            recv_sem=recv_sem,
            device_id=target,
            device_id_type=MESH,
        )
        if when is None:
            copy.start()
        else:
            pl.when(when)(copy.start)

    def arrived(ref, recv_sem):
        pltpu.make_async_remote_copy(
            src_ref=ref,
            dst_ref=ref,
            send_sem=a_send.at[4],
            recv_sem=recv_sem,
            device_id=sibling,
            device_id_type=MESH,
        ).wait_recv()

    def side(r):
        return half if r == 0 else 1 - half

    inner_steps = (0, -1, 1, 2)

    def slot(f, r, do, di):
        inner, outer = place[f]
        return gathered.at[f, side(r), up(outer, do, RING), up(inner, di, RING)]

    def plane_order(k):
        return (k, 1 - k)

    def outer_plane(f, r, j, k, p):
        send(slot(f, r, 0, inner_steps[j]).at[p], a_send.at[2], out_recv.at[r, f, k, j, p],
             ring_device(f, False, (1, -1)[k]))

    def outer_send(f, r, j):
        for n in range(2):
            for k in range(2):
                outer_plane(f, r, j, k, plane_order(k)[n])

    def inner_start(f, r):
        block = slot(f, r, 0, 0)
        for n in range(2):
            for k, step in enumerate((1, -1)):
                p = plane_order(k)[n]
                send(block.at[p], a_send.at[0], in_recv.at[r, f, k, p], ring_device(f, True, step))

    def inner_forward(f, r):
        for k, step in enumerate((1, -1)):
            plane = slot(f, r, 0, -step).at[k]
            arrived(plane, in_recv.at[r, f, k, k])
            send(plane, a_send.at[1], in_recv.at[r, f, k, 2], ring_device(f, True, step))

    def inner_rest(f, r):
        for k, step in enumerate((1, -1)):
            arrived(slot(f, r, 0, -step).at[1 - k], in_recv.at[r, f, k, 1 - k])
            outer_send(f, r, 1 + k)

    def inner_finish(f, r):
        block = slot(f, r, 0, 2)
        for k in range(2):
            arrived(block.at[k], in_recv.at[r, f, k, 2])
        outer_send(f, r, 3)

    def outer_forward(f, r, j):
        for k, step in enumerate((1, -1)):
            plane = slot(f, r, -step, inner_steps[j]).at[k]
            arrived(plane, out_recv.at[r, f, k, j, k])
            send(plane, a_send.at[3], out_recv.at[r, f, k, j, 2], ring_device(f, False, step))

    def outer_rest(f, r, j):
        for k, step in enumerate((1, -1)):
            arrived(slot(f, r, -step, inner_steps[j]).at[1 - k], out_recv.at[r, f, k, j, 1 - k])

    def outer_finish(f, r, j):
        block = slot(f, r, 2, inner_steps[j])
        for k in range(2):
            arrived(block.at[k], out_recv.at[r, f, k, j, 2])

    diagonal = low == y
    owner = jnp.logical_and(diagonal, core == half)
    outer_steps = (0, -1, 1, 2)

    def half_of(d):
        return lax.div(up(z, d, LINE), 4)

    def b_slot(f, h, rel):
        return partner.at[f, h, up(place[f][1], outer_steps[rel], RING)]

    def b_targets():
        for k, step in enumerate((1, -1)):
            fits = [half_of(d * step) == core for d in (1, 2, 3)]
            nearest = jnp.where(fits[0], 1, jnp.where(fits[1], 2, 3))
            found = jnp.logical_or(fits[0], jnp.logical_or(fits[1], fits[2]))
            third = jnp.logical_and(fits[0], fits[2])
            yield k, 0, nearest * step, jnp.logical_and(diagonal, found)
            yield k, 1, 3 * step, jnp.logical_and(diagonal, third)

    def b_start(f, rel, j):
        inner, outer = place[f]
        outer = up(outer, outer_steps[rel], RING)
        inner = up(inner, inner_steps[j], RING)
        piece = gathered.at[f, half, outer, inner, :, :, lanes]
        landing = partner.at[f, half, outer, inner]
        for k, n, distance, when in b_targets():
            target = device(x, y, lax.rem(z + distance + LINE, LINE), f)
            send(piece, b_send.at[k, n], b_recv.at[half, f, rel], target, landing=landing, when=when)

    def b_local(f, r, rel, j):
        inner, outer = place[f]
        outer = up(outer, outer_steps[rel], RING)
        inner = up(inner, inner_steps[j], RING)

        @pl.when(owner)
        def _():
            partner[f, side(r), outer, inner] = gathered[f, side(r), outer, inner, :, :, lanes]

        send(gathered.at[f, side(r), outer, inner, :, :, lanes], b_side.at[0],
             b_recv.at[side(r), f, rel], sibling, landing=partner.at[f, side(r), outer, inner], when=owner)

    def b_wait(f, r, rel):
        arrived(b_slot(f, side(r), rel), b_recv.at[side(r), f, rel])

    def b_place(r):
        distance = lax.rem(z - (y + 4 * side(r)) + 2 * LINE, LINE)
        step = jnp.where(distance < 4, 1, -1)
        steps = jnp.where(distance < 4, distance, LINE - distance)
        before = lax.rem(z - step + LINE, LINE)
        after = lax.rem(z + step + LINE, LINE)
        nearest = jnp.logical_or(steps == 1, lax.div(before, 4) != half)
        goes_on = jnp.logical_and(nearest, jnp.logical_and(steps != 3, lax.div(after, 4) == half))
        return nearest, goes_on, after

    def b_mine(f, r, nearest):
        is_nearest, goes_on, after = b_place(r)
        mine = jnp.logical_and(jnp.logical_not(diagonal), core == f)
        mine = jnp.logical_and(mine, is_nearest if nearest else jnp.logical_not(is_nearest))
        return mine, jnp.logical_and(mine, goes_on), after

    def b_pass_on(f, r, rel, nearest):
        h = side(r)
        block = b_slot(f, h, rel)
        mine, goes_on, after = b_mine(f, r, nearest)
        pl.when(mine)(functools.partial(b_wait, f, r, rel))
        if nearest:
            send(block, b_pass.at[r, f], b_recv.at[h, f, rel], device(x, y, after, core), when=goes_on)
        send(block, b_far.at[int(nearest), r, f], b_recv.at[h, f, rel], sibling, when=mine)

    def b_need(f, r, rel):
        needed = jnp.logical_or(jnp.logical_and(diagonal, core != half), jnp.logical_and(jnp.logical_not(diagonal), core != f))
        pl.when(needed)(functools.partial(b_wait, f, r, rel))

    def chunk(f, r, rel, first=False, last=False):
        h = side(r)
        outer = up(place[f][1], outer_steps[rel], RING)
        depth = RING * 2 * windows
        block = partner[f, h, outer]
        turned = jnp.stack([-block[:, 1], block[:, 0]], axis=1)
        right = jnp.concatenate([block.reshape(depth, width), turned.reshape(depth, width)], axis=1)
        left = gathered[f, h, outer].reshape(depth, gathered.shape[-1])
        product = lax.dot_general(
            left, right, (((0,), (0,)), ((), ())), preferred_element_type=jnp.float32
        )
        for p in range(2):
            part = product[:, p * width:(p + 1) * width]
            if not first:
                part = out[p, f] + part
            if last:
                part = part * norm
            out[p, f] = part

    both = range(2)

    def b_nearest(*rels):
        for rel in rels:
            for f in both:
                for r in both:
                    b_pass_on(f, r, rel, True)

    def b_rest(*rels):
        for rel in rels:
            for f in both:
                for r in both:
                    b_pass_on(f, r, rel, False)

    def work(r, rel, **ends):
        for f in both:
            b_need(f, r, rel)
            chunk(f, r, rel, **ends)

    for f in both:
        send(slot(f, 0, 0, 0), a_send.at[4], z_recv.at[f], device(x, y, up(z, 4, LINE), core))
    for f in both:
        inner_start(f, 0)
    for f in both:
        outer_send(f, 0, 0)
    for f in both:
        inner_forward(f, 0)
    for f in both:
        inner_rest(f, 0)
    for f in both:
        inner_finish(f, 0)
        b_start(f, 0, 0)
        b_local(f, 0, 0, 0)
        b_start(f, 0, 1)
        b_local(f, 0, 0, 1)
        b_start(f, 0, 2)
        b_local(f, 0, 0, 2)
        b_start(f, 0, 3)
        b_local(f, 0, 0, 3)
    for f in both:
        outer_forward(f, 0, 0)
    for f in both:
        outer_rest(f, 0, 0)
        b_start(f, 1, 0)
        b_local(f, 0, 1, 0)
        b_start(f, 2, 0)
        b_local(f, 0, 2, 0)
    for f in both:
        outer_forward(f, 0, 1)
    for f in both:
        outer_rest(f, 0, 1)
        b_start(f, 1, 1)
        b_local(f, 0, 1, 1)
        b_start(f, 2, 1)
        b_local(f, 0, 2, 1)
    for f in both:
        arrived(slot(f, 1, 0, 0), z_recv.at[f])
        inner_start(f, 1)
        outer_send(f, 1, 0)
    for f in both:
        outer_forward(f, 0, 2)
    for f in both:
        outer_rest(f, 0, 2)
        b_start(f, 1, 2)
        b_local(f, 0, 1, 2)
        b_start(f, 2, 2)
        b_local(f, 0, 2, 2)
    b_nearest(0)
    for f in both:
        outer_forward(f, 0, 3)
    for f in both:
        outer_rest(f, 0, 3)
        b_start(f, 1, 3)
        b_local(f, 0, 1, 3)
        b_start(f, 2, 3)
        b_local(f, 0, 2, 3)
    for f in both:
        inner_forward(f, 1)
    for f in both:
        inner_rest(f, 1)
    for f in both:
        outer_finish(f, 0, 0)
        b_start(f, 3, 0)
        b_local(f, 0, 3, 0)
        outer_finish(f, 0, 1)
        b_start(f, 3, 1)
        b_local(f, 0, 3, 1)
        outer_finish(f, 0, 2)
        b_start(f, 3, 2)
        b_local(f, 0, 3, 2)
        outer_finish(f, 0, 3)
        b_start(f, 3, 3)
        b_local(f, 0, 3, 3)
    b_rest(0)
    for f in both:
        inner_finish(f, 1)
    for f in both:
        b_local(f, 1, 0, 0)
        b_local(f, 1, 0, 1)
        b_local(f, 1, 0, 2)
        b_local(f, 1, 0, 3)
    for f in both:
        outer_forward(f, 1, 0)
    for f in both:
        outer_forward(f, 1, 1)
    for f in both:
        outer_rest(f, 1, 0)
        b_local(f, 1, 1, 0)
        b_local(f, 1, 2, 0)
    b_nearest(1)
    b_nearest(2)
    work(0, 0, first=True)
    work(1, 0)
    for f in both:
        outer_forward(f, 1, 2)
    for f in both:
        outer_rest(f, 1, 1)
        b_local(f, 1, 1, 1)
        b_local(f, 1, 2, 1)
    b_rest(1)
    b_rest(2)
    b_nearest(3)
    for f in both:
        outer_forward(f, 1, 3)
    for f in both:
        outer_rest(f, 1, 2)
        b_local(f, 1, 1, 2)
        b_local(f, 1, 2, 2)
    for f in both:
        outer_rest(f, 1, 3)
        b_local(f, 1, 1, 3)
        b_local(f, 1, 2, 3)
    work(0, 1)
    b_rest(3)
    work(0, 2)
    work(0, 3)
    work(1, 1)
    work(1, 2)
    for f in both:
        outer_finish(f, 1, 0)
        b_local(f, 1, 3, 0)
        outer_finish(f, 1, 1)
        b_local(f, 1, 3, 1)
        outer_finish(f, 1, 2)
        b_local(f, 1, 3, 2)
        outer_finish(f, 1, 3)
        b_local(f, 1, 3, 3)
    work(1, 3, last=True)

    def drain(ref, send_sem, when=None):
        wait = pltpu.make_async_remote_copy(
            src_ref=ref,
            dst_ref=ref,
            send_sem=send_sem,
            recv_sem=z_recv.at[0],
            device_id=sibling,
            device_id_type=MESH,
        ).wait_send
        if when is None:
            wait()
        else:
            pl.when(when)(wait)

    drain(gathered.at[0, 0, pl.ds(0, 2)], a_send.at[0])
    drain(gathered.at[0, 0, 0], a_send.at[1])
    drain(gathered.at[0], a_send.at[2])
    drain(gathered.at[0, 0], a_send.at[3])
    drain(gathered.at[0, 0, 0, pl.ds(0, 2)], a_send.at[4])
    drain(partner, b_side.at[0], owner)
    for k, n, _, when in b_targets():
        drain(partner.at[0], b_send.at[k, n], when)
    for r in both:
        for f in both:
            for nearest in (True, False):
                mine, goes_on, _ = b_mine(f, r, nearest)
                drain(partner.at[0, 0], b_far.at[int(nearest), r, f], mine)
                if nearest:
                    drain(partner.at[0, 0], b_pass.at[r, f], goes_on)


def on_device(spectra, valid):
    planes, windows, rows = spectra.shape
    width = rows // 4
    total = windows * lax.axis_size("col")
    norm = 1.0 / float(total) ** 0.5
    dma = pltpu.SemaphoreType.DMA
    vmem = pl.BlockSpec(memory_space=pltpu.VMEM)
    return pl.pallas_call(
        functools.partial(kernel, norm),
        out_shape=jax.ShapeDtypeStruct((2, planes // 2, rows, width), jnp.float32),
        in_specs=[vmem, vmem],
        out_specs=vmem,
        scratch_shapes=[
            pltpu.VMEM((2, 2, RING, RING, 2, windows, rows), jnp.bfloat16),
            pltpu.VMEM((2, 2, RING, RING, 2, windows, width), jnp.bfloat16),
            dma((5,)),
            dma((2,)),
            dma((2, 2, 2, 3)),
            dma((2, 2, 2, 4, 3)),
            dma((2, 2)),
            dma((2, 2)),
            dma((2, 2, 2)),
            dma((1,)),
            dma((2, 2, 4)),
        ],
        compiler_params=pltpu.CompilerParams(
            collective_id=0, has_side_effects=True, vmem_limit_bytes=48 * 2**20
        ),
        cost_estimate=pl.CostEstimate(
            flops=16 * total * rows * width, bytes_accessed=2**22, transcendentals=0
        ),
    )(spectra, valid)


def solution(mesh):
    placed = (P(None, "col", "row"), P("col", "row"))
    return jax.shard_map(
        on_device,
        mesh=mesh,
        in_specs=placed,
        out_specs=P(None, None, "row", "col"),
        check_vma=False,
    )
```

```python
import functools

import jax
import jax.numpy as jnp
from jax import lax
from jax.experimental import pallas as pl
from jax.experimental.pallas import tpu as pltpu
from jax.sharding import PartitionSpec as P

MESH = pl.DeviceIdType.MESH
RING = 4
LINE = 8


def device(x, y, z, core):
    return (lax.rem(z, 4) * 2 + core, y * 8 + lax.div(z, 4) * 4 + x)


def up(a, d, n):
    return lax.rem(a + (d + n), n)


def kernel(norm, spectra, valid, out, gathered, partner, a_send, z_recv, in_recv, far_recv,
           out_recv, rest_recv, last_recv, b_send, b_pass, b_far, b_side, b_recv):
    row = lax.axis_index("row")
    col = lax.axis_index("col")
    core = lax.rem(row, 2)
    low = lax.div(row, 2)
    x = lax.rem(col, 4)
    half = lax.rem(lax.div(col, 4), 2)
    y = lax.div(col, 8)
    z = half * 4 + low
    width = partner.shape[-1]
    windows = spectra.shape[1]
    lanes = pl.ds(pl.multiple_of(x * width, width), width)
    place = ((x, y), (y, x))

    def ring_device(f, inner, step):
        if (f == 0) == inner:
            return device(up(x, step, RING), y, z, core)
        return device(x, up(y, step, RING), z, core)

    sibling = device(x, y, z, 1 - core)

    barrier = pltpu.get_barrier_semaphore()
    diagonal = low == y
    owner = jnp.logical_and(diagonal, core == half)

    def greet(other, when=None):
        signal = functools.partial(
            pl.semaphore_signal, barrier, inc=1, device_id=other, device_id_type=MESH
        )
        if when is None:
            signal()
        else:
            pl.when(when)(signal)

    def half_of(d):
        return lax.div(up(z, d, LINE), 4)

    def b_place(h):
        distance = lax.rem(z - (y + 4 * h) + 2 * LINE, LINE)
        step = jnp.where(distance < 4, 1, -1)
        steps = jnp.where(distance < 4, distance, LINE - distance)
        before = lax.rem(z - step + LINE, LINE)
        second = lax.rem(z - 2 * step + LINE, LINE)
        after = lax.rem(z + step + LINE, LINE)
        nearest = jnp.logical_or(steps == 1, lax.div(before, 4) != half)
        goes_on = jnp.logical_and(nearest, jnp.logical_and(steps != 3, lax.div(after, 4) == half))
        straight = jnp.logical_or(nearest, jnp.logical_and(steps == 3, lax.div(second, 4) == half))
        return nearest, goes_on, straight, before, after

    def b_targets():
        for k, step in enumerate((1, -1)):
            fits = [half_of(d * step) == core for d in (1, 2, 3)]
            nearest = jnp.where(fits[0], 1, jnp.where(fits[1], 2, 3))
            found = jnp.logical_or(fits[0], jnp.logical_or(fits[1], fits[2]))
            third = jnp.logical_and(fits[0], fits[2])
            yield k, 0, nearest * step, jnp.logical_and(diagonal, found)
            yield k, 1, 3 * step, jnp.logical_and(diagonal, third)

    off_diagonal = jnp.logical_not(diagonal)
    for inner in (True, False):
        for step in (1, -1):
            greet(ring_device(0, inner, step))
    greet(device(x, y, up(z, 4, LINE), core))
    greet(sibling, jnp.logical_not(owner))
    copies_to = 5 + jnp.where(jnp.logical_or(off_diagonal, owner), 1, 0)
    for h in range(2):
        _, goes_on, straight, before, _ = b_place(h)
        sender = device(x, y, jnp.where(straight, y + 4 * h, before), jnp.where(straight, half, core))
        greet(sender, off_diagonal)
        copies_to += jnp.where(jnp.logical_and(off_diagonal, goes_on), 1, 0)
    for _, _, _, found in b_targets():
        copies_to += jnp.where(found, 2, 0)

    for f in range(2):
        real = spectra[2 * f].astype(jnp.float32)
        imag = spectra[2 * f + 1].astype(jnp.float32)
        amplitude = jnp.sqrt(real * real + imag * imag)
        factor = valid[...].astype(jnp.float32) / jnp.maximum(amplitude, 0.5)
        inner, outer = place[f]
        gathered[f, half, outer, inner, 0] = (real * factor).astype(jnp.bfloat16)
        gathered[f, half, outer, inner, 1] = (imag * factor).astype(jnp.bfloat16)
    pl.semaphore_wait(barrier, copies_to)

    def send(ref, send_sem, recv_sem, target, landing=None, when=None):
        copy = pltpu.make_async_remote_copy(
            src_ref=ref,
            dst_ref=ref if landing is None else landing,
            send_sem=send_sem,
            recv_sem=recv_sem,
            device_id=target,
            device_id_type=MESH,
        )
        if when is None:
            copy.start()
        else:
            pl.when(when)(copy.start)

    def arrived(ref, recv_sem):
        pltpu.make_async_remote_copy(
            src_ref=ref,
            dst_ref=ref,
            send_sem=a_send.at[4],
            recv_sem=recv_sem,
            device_id=sibling,
            device_id_type=MESH,
        ).wait_recv()

    def side(r):
        return half if r == 0 else 1 - half

    inner_steps = (0, -1, 1, 2)

    def slot(f, r, do, di):
        inner, outer = place[f]
        return gathered.at[f, side(r), up(outer, do, RING), up(inner, di, RING)]

    def plane_order(k):
        return (k, 1 - k)

    def outer_plane(f, r, j, k, p):
        recv_sem = out_recv.at[r, f, k, j] if p == k else rest_recv.at[r, f, j]
        send(slot(f, r, 0, inner_steps[j]).at[p], a_send.at[2], recv_sem,
             ring_device(f, False, (1, -1)[k]))

    def outer_send(f, r, j):
        for n in range(2):
            for k in range(2):
                outer_plane(f, r, j, k, plane_order(k)[n])

    def inner_start(f, r):
        block = slot(f, r, 0, 0)
        for n in range(2):
            for k, step in enumerate((1, -1)):
                p = plane_order(k)[n]
                send(block.at[p], a_send.at[0], in_recv.at[r, f, k, p], ring_device(f, True, step))

    def inner_forward(f, r):
        for k, step in enumerate((1, -1)):
            plane = slot(f, r, 0, -step).at[k]
            arrived(plane, in_recv.at[r, f, k, k])
            send(plane, a_send.at[1], far_recv.at[r, f], ring_device(f, True, step))

    def inner_rest(f, r):
        for k, step in enumerate((1, -1)):
            arrived(slot(f, r, 0, -step).at[1 - k], in_recv.at[r, f, k, 1 - k])
            outer_send(f, r, 1 + k)

    def inner_finish(f, r):
        block = slot(f, r, 0, 2)
        arrived(block, far_recv.at[r, f])
        outer_send(f, r, 3)

    def outer_forward(f, r, j):
        for k, step in enumerate((1, -1)):
            plane = slot(f, r, -step, inner_steps[j]).at[k]
            arrived(plane, out_recv.at[r, f, k, j])
            send(plane, a_send.at[3], last_recv.at[r, f, j], ring_device(f, False, step))

    def outer_rest(f, r, j):
        arrived(slot(f, r, -1, inner_steps[j]), rest_recv.at[r, f, j])

    def outer_finish(f, r, j):
        arrived(slot(f, r, 2, inner_steps[j]), last_recv.at[r, f, j])

    outer_steps = (0, -1, 1, 2)

    def b_slot(f, h, rel):
        return partner.at[f, h, up(place[f][1], outer_steps[rel], RING)]

    def b_start(f, rel, j):
        inner, outer = place[f]
        outer = up(outer, outer_steps[rel], RING)
        inner = up(inner, inner_steps[j], RING)
        piece = gathered.at[f, half, outer, inner, :, :, lanes]
        landing = partner.at[f, half, outer, inner]
        for k, n, distance, when in b_targets():
            target = device(x, y, lax.rem(z + distance + LINE, LINE), f)
            send(piece, b_send.at[k, n], b_recv.at[half, f, rel], target, landing=landing, when=when)

    def b_local(f, r, rel, j):
        inner, outer = place[f]
        outer = up(outer, outer_steps[rel], RING)
        inner = up(inner, inner_steps[j], RING)

        @pl.when(owner)
        def _():
            partner[f, side(r), outer, inner] = gathered[f, side(r), outer, inner, :, :, lanes]

        send(gathered.at[f, side(r), outer, inner, :, :, lanes], b_side.at[0],
             b_recv.at[side(r), f, rel], sibling, landing=partner.at[f, side(r), outer, inner], when=owner)

    def b_wait(f, r, rel):
        arrived(b_slot(f, side(r), rel), b_recv.at[side(r), f, rel])

    def b_mine(f, r, nearest):
        is_nearest, goes_on, _, _, after = b_place(side(r))
        mine = jnp.logical_and(off_diagonal, core == f)
        mine = jnp.logical_and(mine, is_nearest if nearest else jnp.logical_not(is_nearest))
        return mine, jnp.logical_and(mine, goes_on), after

    def b_pass_on(f, r, rel, nearest):
        h = side(r)
        block = b_slot(f, h, rel)
        mine, goes_on, after = b_mine(f, r, nearest)
        pl.when(mine)(functools.partial(b_wait, f, r, rel))
        if nearest:
            send(block, b_pass.at[r, f], b_recv.at[h, f, rel], device(x, y, after, core), when=goes_on)
        send(block, b_far.at[int(nearest), r, f], b_recv.at[h, f, rel], sibling, when=mine)

    def b_need(f, r, rel):
        needed = jnp.logical_or(jnp.logical_and(diagonal, core != half), jnp.logical_and(jnp.logical_not(diagonal), core != f))
        pl.when(needed)(functools.partial(b_wait, f, r, rel))

    def chunk(f, r, rel, first=False, last=False):
        h = side(r)
        outer = up(place[f][1], outer_steps[rel], RING)
        depth = RING * 2 * windows
        block = partner[f, h, outer]
        turned = jnp.stack([-block[:, 1], block[:, 0]], axis=1)
        right = jnp.concatenate([block.reshape(depth, width), turned.reshape(depth, width)], axis=1)
        left = gathered[f, h, outer].reshape(depth, gathered.shape[-1])
        product = lax.dot_general(
            left, right, (((0,), (0,)), ((), ())), preferred_element_type=jnp.float32
        )
        for p in range(2):
            part = product[:, p * width:(p + 1) * width]
            if not first:
                part = out[p, f] + part
            if last:
                part = part * norm
            out[p, f] = part

    both = range(2)

    def b_nearest(*rels):
        for rel in rels:
            for f in both:
                for r in both:
                    b_pass_on(f, r, rel, True)

    def b_rest(*rels):
        for rel in rels:
            for f in both:
                for r in both:
                    b_pass_on(f, r, rel, False)

    def work(r, rel, **ends):
        for f in both:
            b_need(f, r, rel)
            chunk(f, r, rel, **ends)

    for f in both:
        send(slot(f, 0, 0, 0), a_send.at[4], z_recv.at[f], device(x, y, up(z, 4, LINE), core))
    for f in both:
        inner_start(f, 0)
    for f in both:
        outer_send(f, 0, 0)
    for f in both:
        inner_forward(f, 0)
    for f in both:
        inner_rest(f, 0)
    for f in both:
        inner_finish(f, 0)
        b_start(f, 0, 0)
        b_local(f, 0, 0, 0)
        b_start(f, 0, 1)
        b_local(f, 0, 0, 1)
        b_start(f, 0, 2)
        b_local(f, 0, 0, 2)
        b_start(f, 0, 3)
        b_local(f, 0, 0, 3)
    for f in both:
        outer_forward(f, 0, 0)
    for f in both:
        outer_rest(f, 0, 0)
        b_start(f, 1, 0)
        b_local(f, 0, 1, 0)
        b_start(f, 2, 0)
        b_local(f, 0, 2, 0)
    for f in both:
        outer_forward(f, 0, 1)
    for f in both:
        outer_rest(f, 0, 1)
        b_start(f, 1, 1)
        b_local(f, 0, 1, 1)
        b_start(f, 2, 1)
        b_local(f, 0, 2, 1)
    for f in both:
        arrived(slot(f, 1, 0, 0), z_recv.at[f])
        inner_start(f, 1)
        outer_send(f, 1, 0)
    for f in both:
        outer_forward(f, 0, 2)
    for f in both:
        outer_rest(f, 0, 2)
        b_start(f, 1, 2)
        b_local(f, 0, 1, 2)
        b_start(f, 2, 2)
        b_local(f, 0, 2, 2)
    b_nearest(0)
    for f in both:
        outer_forward(f, 0, 3)
    for f in both:
        outer_rest(f, 0, 3)
        b_start(f, 1, 3)
        b_local(f, 0, 1, 3)
        b_start(f, 2, 3)
        b_local(f, 0, 2, 3)
    for f in both:
        inner_forward(f, 1)
    for f in both:
        inner_rest(f, 1)
    for f in both:
        outer_finish(f, 0, 0)
        b_start(f, 3, 0)
        b_local(f, 0, 3, 0)
        outer_finish(f, 0, 1)
        b_start(f, 3, 1)
        b_local(f, 0, 3, 1)
        outer_finish(f, 0, 2)
        b_start(f, 3, 2)
        b_local(f, 0, 3, 2)
        outer_finish(f, 0, 3)
        b_start(f, 3, 3)
        b_local(f, 0, 3, 3)
    b_rest(0)
    for f in both:
        inner_finish(f, 1)
    for f in both:
        b_local(f, 1, 0, 0)
        b_local(f, 1, 0, 1)
        b_local(f, 1, 0, 2)
        b_local(f, 1, 0, 3)
    for f in both:
        outer_forward(f, 1, 0)
    for f in both:
        outer_forward(f, 1, 1)
    for f in both:
        outer_rest(f, 1, 0)
        b_local(f, 1, 1, 0)
        b_local(f, 1, 2, 0)
    b_nearest(1)
    b_nearest(2)
    work(0, 0, first=True)
    work(1, 0)
    for f in both:
        outer_forward(f, 1, 2)
    for f in both:
        outer_rest(f, 1, 1)
        b_local(f, 1, 1, 1)
        b_local(f, 1, 2, 1)
    b_rest(1)
    b_rest(2)
    b_nearest(3)
    for f in both:
        outer_forward(f, 1, 3)
    for f in both:
        outer_rest(f, 1, 2)
        b_local(f, 1, 1, 2)
        b_local(f, 1, 2, 2)
    for f in both:
        outer_rest(f, 1, 3)
        b_local(f, 1, 1, 3)
        b_local(f, 1, 2, 3)
    work(0, 1)
    b_rest(3)
    work(0, 2)
    work(0, 3)
    work(1, 1)
    work(1, 2)
    for f in both:
        outer_finish(f, 1, 0)
        b_local(f, 1, 3, 0)
        outer_finish(f, 1, 1)
        b_local(f, 1, 3, 1)
        outer_finish(f, 1, 2)
        b_local(f, 1, 3, 2)
        outer_finish(f, 1, 3)
        b_local(f, 1, 3, 3)
    work(1, 3, last=True)

    def drain(ref, send_sem, when=None):
        wait = pltpu.make_async_remote_copy(
            src_ref=ref,
            dst_ref=ref,
            send_sem=send_sem,
            recv_sem=z_recv.at[0],
            device_id=sibling,
            device_id_type=MESH,
        ).wait_send
        if when is None:
            wait()
        else:
            pl.when(when)(wait)

    drain(gathered.at[0, 0, pl.ds(0, 2)], a_send.at[0])
    drain(gathered.at[0, 0, 0], a_send.at[1])
    drain(gathered.at[0], a_send.at[2])
    drain(gathered.at[0, 0], a_send.at[3])
    drain(gathered.at[0, 0, 0, pl.ds(0, 2)], a_send.at[4])
    drain(partner, b_side.at[0], owner)
    for k, n, _, when in b_targets():
        drain(partner.at[0], b_send.at[k, n], when)
    for r in both:
        for f in both:
            for nearest in (True, False):
                mine, goes_on, _ = b_mine(f, r, nearest)
                drain(partner.at[0, 0], b_far.at[int(nearest), r, f], mine)
                if nearest:
                    drain(partner.at[0, 0], b_pass.at[r, f], goes_on)


def on_device(spectra, valid):
    planes, windows, rows = spectra.shape
    width = rows // 4
    total = windows * lax.axis_size("col")
    norm = 1.0 / float(total) ** 0.5
    dma = pltpu.SemaphoreType.DMA
    vmem = pl.BlockSpec(memory_space=pltpu.VMEM)
    return pl.pallas_call(
        functools.partial(kernel, norm),
        out_shape=jax.ShapeDtypeStruct((2, planes // 2, rows, width), jnp.float32),
        in_specs=[vmem, vmem],
        out_specs=vmem,
        scratch_shapes=[
            pltpu.VMEM((2, 2, RING, RING, 2, windows, rows), jnp.bfloat16),
            pltpu.VMEM((2, 2, RING, RING, 2, windows, width), jnp.bfloat16),
            dma((5,)),
            dma((2,)),
            dma((2, 2, 2, 2)),
            dma((2, 2)),
            dma((2, 2, 2, 4)),
            dma((2, 2, 4)),
            dma((2, 2, 4)),
            dma((2, 2)),
            dma((2, 2)),
            dma((2, 2, 2)),
            dma((1,)),
            dma((2, 2, 4)),
        ],
        compiler_params=pltpu.CompilerParams(
            collective_id=0, has_side_effects=True, vmem_limit_bytes=48 * 2**20
        ),
        cost_estimate=pl.CostEstimate(
            flops=16 * total * rows * width, bytes_accessed=2**22, transcendentals=0
        ),
    )(spectra, valid)


def solution(mesh):
    placed = (P(None, "col", "row"), P("col", "row"))
    return jax.shard_map(
        on_device,
        mesh=mesh,
        in_specs=placed,
        out_specs=P(None, None, "row", "col"),
        check_vma=False,
    )
```

```python
import functools

import jax
import jax.numpy as jnp
from jax import lax
from jax.experimental import pallas as pl
from jax.experimental.pallas import tpu as pltpu
from jax.sharding import PartitionSpec as P

MESH = pl.DeviceIdType.MESH
RING = 4
LINE = 8


def device(x, y, z, core):
    return (lax.rem(z, 4) * 2 + core, y * 8 + lax.div(z, 4) * 4 + x)


def up(a, d, n):
    return lax.rem(a + (d + n), n)


def kernel(norm, white_a, white_b, white_c, white_d, out, gathered, partner, a_send, z_recv, in_recv, far_recv,
           out_recv, rest_recv, last_recv, b_send, b_pass, b_far, b_side, b_recv):
    row = lax.axis_index("row")
    col = lax.axis_index("col")
    core = lax.rem(row, 2)
    low = lax.div(row, 2)
    x = lax.rem(col, 4)
    half = lax.rem(lax.div(col, 4), 2)
    y = lax.div(col, 8)
    z = half * 4 + low
    width = partner.shape[-1]
    windows = white_a.shape[0]
    lanes = pl.ds(pl.multiple_of(x * width, width), width)
    place = ((x, y), (y, x))

    def ring_device(f, inner, step):
        if (f == 0) == inner:
            return device(up(x, step, RING), y, z, core)
        return device(x, up(y, step, RING), z, core)

    sibling = device(x, y, z, 1 - core)

    barrier = pltpu.get_barrier_semaphore()
    diagonal = low == y
    owner = jnp.logical_and(diagonal, core == half)

    def greet(other, when=None):
        signal = functools.partial(
            pl.semaphore_signal, barrier, inc=1, device_id=other, device_id_type=MESH
        )
        if when is None:
            signal()
        else:
            pl.when(when)(signal)

    def half_of(d):
        return lax.div(up(z, d, LINE), 4)

    def b_place(h):
        distance = lax.rem(z - (y + 4 * h) + 2 * LINE, LINE)
        step = jnp.where(distance < 4, 1, -1)
        steps = jnp.where(distance < 4, distance, LINE - distance)
        before = lax.rem(z - step + LINE, LINE)
        second = lax.rem(z - 2 * step + LINE, LINE)
        after = lax.rem(z + step + LINE, LINE)
        nearest = jnp.logical_or(steps == 1, lax.div(before, 4) != half)
        goes_on = jnp.logical_and(nearest, jnp.logical_and(steps != 3, lax.div(after, 4) == half))
        straight = jnp.logical_or(nearest, jnp.logical_and(steps == 3, lax.div(second, 4) == half))
        return nearest, goes_on, straight, before, after

    def b_targets():
        for k, step in enumerate((1, -1)):
            fits = [half_of(d * step) == core for d in (1, 2, 3)]
            nearest = jnp.where(fits[0], 1, jnp.where(fits[1], 2, 3))
            found = jnp.logical_or(fits[0], jnp.logical_or(fits[1], fits[2]))
            third = jnp.logical_and(fits[0], fits[2])
            yield k, 0, nearest * step, jnp.logical_and(diagonal, found)
            yield k, 1, 3 * step, jnp.logical_and(diagonal, third)

    off_diagonal = jnp.logical_not(diagonal)
    for inner in (True, False):
        for step in (1, -1):
            greet(ring_device(0, inner, step))
    greet(device(x, y, up(z, 4, LINE), core))
    greet(sibling, jnp.logical_not(owner))
    copies_to = 5 + jnp.where(jnp.logical_or(off_diagonal, owner), 1, 0)
    for h in range(2):
        _, goes_on, straight, before, _ = b_place(h)
        sender = device(x, y, jnp.where(straight, y + 4 * h, before), jnp.where(straight, half, core))
        greet(sender, off_diagonal)
        copies_to += jnp.where(jnp.logical_and(off_diagonal, goes_on), 1, 0)
    for _, _, _, found in b_targets():
        copies_to += jnp.where(found, 2, 0)

    for f, planes in enumerate(((white_a, white_b), (white_c, white_d))):
        inner, outer = place[f]
        for p in range(2):
            gathered[f, half, outer, inner, p] = planes[p][...]
    pl.semaphore_wait(barrier, copies_to)

    def send(ref, send_sem, recv_sem, target, landing=None, when=None):
        copy = pltpu.make_async_remote_copy(
            src_ref=ref,
            dst_ref=ref if landing is None else landing,
            send_sem=send_sem,
            recv_sem=recv_sem,
            device_id=target,
            device_id_type=MESH,
        )
        if when is None:
            copy.start()
        else:
            pl.when(when)(copy.start)

    def arrived(ref, recv_sem):
        pltpu.make_async_remote_copy(
            src_ref=ref,
            dst_ref=ref,
            send_sem=a_send.at[4],
            recv_sem=recv_sem,
            device_id=sibling,
            device_id_type=MESH,
        ).wait_recv()

    def side(r):
        return half if r == 0 else 1 - half

    inner_steps = (0, -1, 1, 2)

    def slot(f, r, do, di):
        inner, outer = place[f]
        return gathered.at[f, side(r), up(outer, do, RING), up(inner, di, RING)]

    def plane_order(k):
        return (k, 1 - k)

    def outer_plane(f, r, j, k, p):
        recv_sem = out_recv.at[r, f, k, j] if p == k else rest_recv.at[r, f, j]
        send(slot(f, r, 0, inner_steps[j]).at[p], a_send.at[2], recv_sem,
             ring_device(f, False, (1, -1)[k]))

    def outer_send(f, r, j):
        for n in range(2):
            for k in range(2):
                outer_plane(f, r, j, k, plane_order(k)[n])

    def inner_start(f, r):
        block = slot(f, r, 0, 0)
        for n in range(2):
            for k, step in enumerate((1, -1)):
                p = plane_order(k)[n]
                send(block.at[p], a_send.at[0], in_recv.at[r, f, k, p], ring_device(f, True, step))

    def inner_forward(f, r):
        for k, step in enumerate((1, -1)):
            plane = slot(f, r, 0, -step).at[k]
            arrived(plane, in_recv.at[r, f, k, k])
            send(plane, a_send.at[1], far_recv.at[r, f], ring_device(f, True, step))

    def inner_rest(f, r):
        for k, step in enumerate((1, -1)):
            arrived(slot(f, r, 0, -step).at[1 - k], in_recv.at[r, f, k, 1 - k])
            outer_send(f, r, 1 + k)

    def inner_finish(f, r):
        block = slot(f, r, 0, 2)
        arrived(block, far_recv.at[r, f])
        outer_send(f, r, 3)

    def outer_forward(f, r, j):
        for k, step in enumerate((1, -1)):
            plane = slot(f, r, -step, inner_steps[j]).at[k]
            arrived(plane, out_recv.at[r, f, k, j])
            send(plane, a_send.at[3], last_recv.at[r, f, j], ring_device(f, False, step))

    def outer_rest(f, r, j):
        arrived(slot(f, r, -1, inner_steps[j]), rest_recv.at[r, f, j])

    def outer_finish(f, r, j):
        arrived(slot(f, r, 2, inner_steps[j]), last_recv.at[r, f, j])

    outer_steps = (0, -1, 1, 2)

    def b_slot(f, h, rel):
        return partner.at[f, h, up(place[f][1], outer_steps[rel], RING)]

    def b_start(f, rel, j):
        inner, outer = place[f]
        outer = up(outer, outer_steps[rel], RING)
        inner = up(inner, inner_steps[j], RING)
        piece = gathered.at[f, half, outer, inner, :, :, lanes]
        landing = partner.at[f, half, outer, inner]
        for k, n, distance, when in b_targets():
            target = device(x, y, lax.rem(z + distance + LINE, LINE), f)
            send(piece, b_send.at[k, n], b_recv.at[half, f, rel], target, landing=landing, when=when)

    def b_local(f, r, rel, j):
        inner, outer = place[f]
        outer = up(outer, outer_steps[rel], RING)
        inner = up(inner, inner_steps[j], RING)

        @pl.when(owner)
        def _():
            partner[f, side(r), outer, inner] = gathered[f, side(r), outer, inner, :, :, lanes]

        send(gathered.at[f, side(r), outer, inner, :, :, lanes], b_side.at[0],
             b_recv.at[side(r), f, rel], sibling, landing=partner.at[f, side(r), outer, inner], when=owner)

    def b_wait(f, r, rel):
        arrived(b_slot(f, side(r), rel), b_recv.at[side(r), f, rel])

    def b_mine(f, r, nearest):
        is_nearest, goes_on, _, _, after = b_place(side(r))
        mine = jnp.logical_and(off_diagonal, core == f)
        mine = jnp.logical_and(mine, is_nearest if nearest else jnp.logical_not(is_nearest))
        return mine, jnp.logical_and(mine, goes_on), after

    def b_pass_on(f, r, rel, nearest):
        h = side(r)
        block = b_slot(f, h, rel)
        mine, goes_on, after = b_mine(f, r, nearest)
        pl.when(mine)(functools.partial(b_wait, f, r, rel))
        if nearest:
            send(block, b_pass.at[r, f], b_recv.at[h, f, rel], device(x, y, after, core), when=goes_on)
        send(block, b_far.at[int(nearest), r, f], b_recv.at[h, f, rel], sibling, when=mine)

    def b_need(f, r, rel):
        needed = jnp.logical_or(jnp.logical_and(diagonal, core != half), jnp.logical_and(jnp.logical_not(diagonal), core != f))
        pl.when(needed)(functools.partial(b_wait, f, r, rel))

    def chunk(f, r, rel, first=False, last=False):
        h = side(r)
        outer = up(place[f][1], outer_steps[rel], RING)
        depth = RING * 2 * windows
        block = partner[f, h, outer]
        turned = jnp.stack([-block[:, 1], block[:, 0]], axis=1)
        right = jnp.concatenate([block.reshape(depth, width), turned.reshape(depth, width)], axis=1)
        left = gathered[f, h, outer].reshape(depth, gathered.shape[-1])
        product = lax.dot_general(
            left, right, (((0,), (0,)), ((), ())), preferred_element_type=jnp.float32
        )
        for p in range(2):
            part = product[:, p * width:(p + 1) * width]
            if not first:
                part = out[p, f] + part
            if last:
                part = part * norm
            out[p, f] = part

    both = range(2)

    def b_nearest(*rels):
        for rel in rels:
            for f in both:
                for r in both:
                    b_pass_on(f, r, rel, True)

    def b_rest(*rels):
        for rel in rels:
            for f in both:
                for r in both:
                    b_pass_on(f, r, rel, False)

    def work(r, rel, **ends):
        for f in both:
            b_need(f, r, rel)
            chunk(f, r, rel, **ends)

    for f in both:
        send(slot(f, 0, 0, 0), a_send.at[4], z_recv.at[f], device(x, y, up(z, 4, LINE), core))
    for f in both:
        inner_start(f, 0)
    for f in both:
        outer_send(f, 0, 0)
    for f in both:
        inner_forward(f, 0)
    for f in both:
        inner_rest(f, 0)
    for f in both:
        inner_finish(f, 0)
        b_start(f, 0, 0)
        b_local(f, 0, 0, 0)
        b_start(f, 0, 1)
        b_local(f, 0, 0, 1)
        b_start(f, 0, 2)
        b_local(f, 0, 0, 2)
        b_start(f, 0, 3)
        b_local(f, 0, 0, 3)
    for f in both:
        outer_forward(f, 0, 0)
    for f in both:
        outer_rest(f, 0, 0)
        b_start(f, 1, 0)
        b_local(f, 0, 1, 0)
        b_start(f, 2, 0)
        b_local(f, 0, 2, 0)
    for f in both:
        outer_forward(f, 0, 1)
    for f in both:
        outer_rest(f, 0, 1)
        b_start(f, 1, 1)
        b_local(f, 0, 1, 1)
        b_start(f, 2, 1)
        b_local(f, 0, 2, 1)
    for f in both:
        arrived(slot(f, 1, 0, 0), z_recv.at[f])
        inner_start(f, 1)
        outer_send(f, 1, 0)
    for f in both:
        outer_forward(f, 0, 2)
    for f in both:
        outer_rest(f, 0, 2)
        b_start(f, 1, 2)
        b_local(f, 0, 1, 2)
        b_start(f, 2, 2)
        b_local(f, 0, 2, 2)
    for f in both:
        outer_forward(f, 0, 3)
    for f in both:
        outer_rest(f, 0, 3)
        b_start(f, 1, 3)
        b_local(f, 0, 1, 3)
        b_start(f, 2, 3)
        b_local(f, 0, 2, 3)
    b_nearest(0)
    for f in both:
        inner_forward(f, 1)
    for f in both:
        inner_rest(f, 1)
    for f in both:
        outer_finish(f, 0, 0)
        b_start(f, 3, 0)
        b_local(f, 0, 3, 0)
        outer_finish(f, 0, 1)
        b_start(f, 3, 1)
        b_local(f, 0, 3, 1)
        outer_finish(f, 0, 2)
        b_start(f, 3, 2)
        b_local(f, 0, 3, 2)
        outer_finish(f, 0, 3)
        b_start(f, 3, 3)
        b_local(f, 0, 3, 3)
    for f in both:
        inner_finish(f, 1)
    for f in both:
        b_local(f, 1, 0, 0)
        b_local(f, 1, 0, 1)
        b_local(f, 1, 0, 2)
        b_local(f, 1, 0, 3)
    for f in both:
        outer_forward(f, 1, 0)
    for f in both:
        outer_forward(f, 1, 1)
    b_rest(0)
    for f in both:
        outer_rest(f, 1, 0)
        b_local(f, 1, 1, 0)
        b_local(f, 1, 2, 0)
    b_nearest(1)
    b_nearest(2)
    for f in both:
        outer_forward(f, 1, 2)
    work(0, 0, first=True)
    work(1, 0)
    for f in both:
        outer_rest(f, 1, 1)
        b_local(f, 1, 1, 1)
        b_local(f, 1, 2, 1)
    b_rest(1)
    b_rest(2)
    b_nearest(3)
    work(0, 1)
    for f in both:
        outer_forward(f, 1, 3)
    work(0, 2)
    for f in both:
        outer_rest(f, 1, 2)
        b_local(f, 1, 1, 2)
        b_local(f, 1, 2, 2)
    for f in both:
        outer_rest(f, 1, 3)
        b_local(f, 1, 1, 3)
        b_local(f, 1, 2, 3)
    b_rest(3)
    work(0, 3)
    work(1, 1)
    work(1, 2)
    for f in both:
        outer_finish(f, 1, 0)
        b_local(f, 1, 3, 0)
        outer_finish(f, 1, 1)
        b_local(f, 1, 3, 1)
        outer_finish(f, 1, 2)
        b_local(f, 1, 3, 2)
        outer_finish(f, 1, 3)
        b_local(f, 1, 3, 3)
    work(1, 3, last=True)

    def drain(ref, send_sem, when=None):
        wait = pltpu.make_async_remote_copy(
            src_ref=ref,
            dst_ref=ref,
            send_sem=send_sem,
            recv_sem=z_recv.at[0],
            device_id=sibling,
            device_id_type=MESH,
        ).wait_send
        if when is None:
            wait()
        else:
            pl.when(when)(wait)

    drain(gathered.at[0, 0, pl.ds(0, 2)], a_send.at[0])
    drain(gathered.at[0, 0, 0], a_send.at[1])
    drain(gathered.at[0], a_send.at[2])
    drain(gathered.at[0, 0], a_send.at[3])
    drain(gathered.at[0, 0, 0, pl.ds(0, 2)], a_send.at[4])
    drain(partner, b_side.at[0], owner)
    for k, n, _, when in b_targets():
        drain(partner.at[0], b_send.at[k, n], when)
    for r in both:
        for f in both:
            for nearest in (True, False):
                mine, goes_on, _ = b_mine(f, r, nearest)
                drain(partner.at[0, 0], b_far.at[int(nearest), r, f], mine)
                if nearest:
                    drain(partner.at[0, 0], b_pass.at[r, f], goes_on)


def whiten(spectra, valid):
    kept = valid.astype(jnp.float32)
    white = []
    for f in range(2):
        real = spectra[2 * f].astype(jnp.float32)
        imag = spectra[2 * f + 1].astype(jnp.float32)
        factor = kept / jnp.maximum(jnp.sqrt(real * real + imag * imag), 0.5)
        white += [(real * factor).astype(jnp.bfloat16), (imag * factor).astype(jnp.bfloat16)]
    return white


def on_device(spectra, valid):
    planes, windows, rows = spectra.shape
    width = rows // 4
    total = windows * lax.axis_size("col")
    norm = 1.0 / float(total) ** 0.5
    dma = pltpu.SemaphoreType.DMA
    vmem = pl.BlockSpec(memory_space=pltpu.VMEM)
    return pl.pallas_call(
        functools.partial(kernel, norm),
        out_shape=jax.ShapeDtypeStruct((2, planes // 2, rows, width), jnp.float32),
        in_specs=[vmem] * 4,
        out_specs=vmem,
        scratch_shapes=[
            pltpu.VMEM((2, 2, RING, RING, 2, windows, rows), jnp.bfloat16),
            pltpu.VMEM((2, 2, RING, RING, 2, windows, width), jnp.bfloat16),
            dma((5,)),
            dma((2,)),
            dma((2, 2, 2, 2)),
            dma((2, 2)),
            dma((2, 2, 2, 4)),
            dma((2, 2, 4)),
            dma((2, 2, 4)),
            dma((2, 2)),
            dma((2, 2)),
            dma((2, 2, 2)),
            dma((1,)),
            dma((2, 2, 4)),
        ],
        compiler_params=pltpu.CompilerParams(
            collective_id=0, has_side_effects=True, vmem_limit_bytes=48 * 2**20
        ),
        cost_estimate=pl.CostEstimate(
            flops=16 * total * rows * width, bytes_accessed=2**22, transcendentals=0
        ),
    )(*whiten(spectra, valid))


def solution(mesh):
    placed = (P(None, "col", "row"), P("col", "row"))
    return jax.shard_map(
        on_device,
        mesh=mesh,
        in_specs=placed,
        out_specs=P(None, None, "row", "col"),
        check_vma=False,
    )
```

```python
import functools

import jax
import jax.numpy as jnp
from jax import lax
from jax.experimental import pallas as pl
from jax.experimental.pallas import tpu as pltpu
from jax.sharding import PartitionSpec as P

MESH = pl.DeviceIdType.MESH
RING = 4
LINE = 8


def device(x, y, z, core):
    return (lax.rem(z, 4) * 2 + core, y * 8 + lax.div(z, 4) * 4 + x)


def up(a, d, n):
    return lax.rem(a + (d + n), n)


def kernel(norm, white_a, white_b, white_c, white_d, out, gathered, partner, a_send, z_recv, in_recv, far_recv,
           out_recv, rest_recv, last_recv, b_send, b_pass, b_far, b_side, b_recv):
    row = lax.axis_index("row")
    col = lax.axis_index("col")
    core = lax.rem(row, 2)
    low = lax.div(row, 2)
    x = lax.rem(col, 4)
    half = lax.rem(lax.div(col, 4), 2)
    y = lax.div(col, 8)
    z = half * 4 + low
    width = partner.shape[-1]
    windows = white_a.shape[0]
    lanes = pl.ds(pl.multiple_of(x * width, width), width)
    place = ((x, y), (y, x))

    def ring_device(f, inner, step):
        if (f == 0) == inner:
            return device(up(x, step, RING), y, z, core)
        return device(x, up(y, step, RING), z, core)

    sibling = device(x, y, z, 1 - core)

    barrier = pltpu.get_barrier_semaphore()
    diagonal = low == y
    owner = jnp.logical_and(diagonal, core == half)

    def greet(other, when=None):
        signal = functools.partial(
            pl.semaphore_signal, barrier, inc=1, device_id=other, device_id_type=MESH
        )
        if when is None:
            signal()
        else:
            pl.when(when)(signal)

    def half_of(d):
        return lax.div(up(z, d, LINE), 4)

    def b_place(h):
        distance = lax.rem(z - (y + 4 * h) + 2 * LINE, LINE)
        step = jnp.where(distance < 4, 1, -1)
        steps = jnp.where(distance < 4, distance, LINE - distance)
        before = lax.rem(z - step + LINE, LINE)
        second = lax.rem(z - 2 * step + LINE, LINE)
        after = lax.rem(z + step + LINE, LINE)
        nearest = jnp.logical_or(steps == 1, lax.div(before, 4) != half)
        goes_on = jnp.logical_and(nearest, jnp.logical_and(steps != 3, lax.div(after, 4) == half))
        straight = jnp.logical_or(nearest, jnp.logical_and(steps == 3, lax.div(second, 4) == half))
        return nearest, goes_on, straight, before, after

    def b_targets():
        for k, step in enumerate((1, -1)):
            fits = [half_of(d * step) == core for d in (1, 2, 3)]
            nearest = jnp.where(fits[0], 1, jnp.where(fits[1], 2, 3))
            found = jnp.logical_or(fits[0], jnp.logical_or(fits[1], fits[2]))
            third = jnp.logical_and(fits[0], fits[2])
            yield k, 0, nearest * step, jnp.logical_and(diagonal, found)
            yield k, 1, 3 * step, jnp.logical_and(diagonal, third)

    off_diagonal = jnp.logical_not(diagonal)
    for inner in (True, False):
        for step in (1, -1):
            greet(ring_device(0, inner, step))
    greet(device(x, y, up(z, 4, LINE), core))
    greet(sibling, jnp.logical_not(owner))
    copies_to = 5 + jnp.where(jnp.logical_or(off_diagonal, owner), 1, 0)
    for h in range(2):
        _, goes_on, straight, before, _ = b_place(h)
        sender = device(x, y, jnp.where(straight, y + 4 * h, before), jnp.where(straight, half, core))
        greet(sender, off_diagonal)
        copies_to += jnp.where(jnp.logical_and(off_diagonal, goes_on), 1, 0)
    for _, _, _, found in b_targets():
        copies_to += jnp.where(found, 2, 0)

    for f, planes in enumerate(((white_a, white_b), (white_c, white_d))):
        inner, outer = place[f]
        for p in range(2):
            gathered[f, half, outer, inner, p] = planes[p][...]
    pl.semaphore_wait(barrier, copies_to)

    def send(ref, send_sem, recv_sem, target, landing=None, when=None):
        copy = pltpu.make_async_remote_copy(
            src_ref=ref,
            dst_ref=ref if landing is None else landing,
            send_sem=send_sem,
            recv_sem=recv_sem,
            device_id=target,
            device_id_type=MESH,
        )
        if when is None:
            copy.start()
        else:
            pl.when(when)(copy.start)

    def arrived(ref, recv_sem):
        pltpu.make_async_remote_copy(
            src_ref=ref,
            dst_ref=ref,
            send_sem=a_send.at[4],
            recv_sem=recv_sem,
            device_id=sibling,
            device_id_type=MESH,
        ).wait_recv()

    def side(r):
        return half if r == 0 else 1 - half

    inner_steps = (0, -1, 1, 2)

    def slot(f, r, do, di):
        inner, outer = place[f]
        return gathered.at[f, side(r), up(outer, do, RING), up(inner, di, RING)]

    def plane_order(k):
        return (k, 1 - k)

    def outer_plane(f, r, j, k, p):
        recv_sem = out_recv.at[r, f, k, j] if p == k else rest_recv.at[r, f, j]
        send(slot(f, r, 0, inner_steps[j]).at[p], a_send.at[2], recv_sem,
             ring_device(f, False, (1, -1)[k]))

    def outer_send(f, r, j):
        for n in range(2):
            for k in range(2):
                outer_plane(f, r, j, k, plane_order(k)[n])

    def inner_start(f, r):
        block = slot(f, r, 0, 0)
        for n in range(2):
            for k, step in enumerate((1, -1)):
                p = plane_order(k)[n]
                send(block.at[p], a_send.at[0], in_recv.at[r, f, k, p], ring_device(f, True, step))

    def inner_forward(f, r):
        for k, step in enumerate((1, -1)):
            plane = slot(f, r, 0, -step).at[k]
            arrived(plane, in_recv.at[r, f, k, k])
            send(plane, a_send.at[1], far_recv.at[r, f], ring_device(f, True, step))

    def inner_rest(f, r):
        for k, step in enumerate((1, -1)):
            arrived(slot(f, r, 0, -step).at[1 - k], in_recv.at[r, f, k, 1 - k])
            outer_send(f, r, 1 + k)

    def inner_finish(f, r):
        block = slot(f, r, 0, 2)
        arrived(block, far_recv.at[r, f])
        outer_send(f, r, 3)

    def outer_forward(f, r, j):
        for k, step in enumerate((1, -1)):
            plane = slot(f, r, -step, inner_steps[j]).at[k]
            arrived(plane, out_recv.at[r, f, k, j])
            send(plane, a_send.at[3], last_recv.at[r, f, j], ring_device(f, False, step))

    def outer_rest(f, r, j):
        arrived(slot(f, r, -1, inner_steps[j]), rest_recv.at[r, f, j])

    def outer_finish(f, r, j):
        arrived(slot(f, r, 2, inner_steps[j]), last_recv.at[r, f, j])

    outer_steps = (0, -1, 1, 2)

    def b_slot(f, h, rel):
        return partner.at[f, h, up(place[f][1], outer_steps[rel], RING)]

    def b_start(f, rel, j):
        inner, outer = place[f]
        outer = up(outer, outer_steps[rel], RING)
        inner = up(inner, inner_steps[j], RING)
        piece = gathered.at[f, half, outer, inner, :, :, lanes]
        landing = partner.at[f, half, outer, inner]
        for k, n, distance, when in b_targets():
            target = device(x, y, lax.rem(z + distance + LINE, LINE), f)
            send(piece, b_send.at[k, n], b_recv.at[half, f, rel], target, landing=landing, when=when)

    def b_local(f, r, rel, j):
        inner, outer = place[f]
        outer = up(outer, outer_steps[rel], RING)
        inner = up(inner, inner_steps[j], RING)

        @pl.when(owner)
        def _():
            partner[f, side(r), outer, inner] = gathered[f, side(r), outer, inner, :, :, lanes]

        send(gathered.at[f, side(r), outer, inner, :, :, lanes], b_side.at[0],
             b_recv.at[side(r), f, rel], sibling, landing=partner.at[f, side(r), outer, inner], when=owner)

    def b_wait(f, r, rel):
        arrived(b_slot(f, side(r), rel), b_recv.at[side(r), f, rel])

    def b_mine(f, r, nearest):
        is_nearest, goes_on, _, _, after = b_place(side(r))
        mine = jnp.logical_and(off_diagonal, core == f)
        mine = jnp.logical_and(mine, is_nearest if nearest else jnp.logical_not(is_nearest))
        return mine, jnp.logical_and(mine, goes_on), after

    def b_pass_on(f, r, rel, nearest):
        h = side(r)
        block = b_slot(f, h, rel)
        mine, goes_on, after = b_mine(f, r, nearest)
        pl.when(mine)(functools.partial(b_wait, f, r, rel))
        if nearest:
            send(block, b_pass.at[r, f], b_recv.at[h, f, rel], device(x, y, after, core), when=goes_on)
        send(block, b_far.at[int(nearest), r, f], b_recv.at[h, f, rel], sibling, when=mine)

    def b_need(f, r, rel):
        needed = jnp.logical_or(jnp.logical_and(diagonal, core != half), jnp.logical_and(jnp.logical_not(diagonal), core != f))
        pl.when(needed)(functools.partial(b_wait, f, r, rel))

    def chunk(f, r, rel, first=False, last=False):
        h = side(r)
        outer = up(place[f][1], outer_steps[rel], RING)
        depth = RING * 2 * windows
        block = partner[f, h, outer]
        turned = jnp.stack([-block[:, 1], block[:, 0]], axis=1)
        right = jnp.concatenate([block.reshape(depth, width), turned.reshape(depth, width)], axis=1)
        left = gathered[f, h, outer].reshape(depth, gathered.shape[-1])
        product = lax.dot_general(
            left, right, (((0,), (0,)), ((), ())), preferred_element_type=jnp.float32
        )
        for p in range(2):
            part = product[:, p * width:(p + 1) * width]
            if not first:
                part = out[p, f] + part
            if last:
                part = part * norm
            out[p, f] = part

    both = range(2)

    def b_nearest(*rels):
        for rel in rels:
            for f in both:
                for r in both:
                    b_pass_on(f, r, rel, True)

    def b_rest(*rels):
        for rel in rels:
            for f in both:
                for r in both:
                    b_pass_on(f, r, rel, False)

    def work(r, rel, **ends):
        for f in both:
            b_need(f, r, rel)
            chunk(f, r, rel, **ends)

    for f in both:
        send(slot(f, 0, 0, 0), a_send.at[4], z_recv.at[f], device(x, y, up(z, 4, LINE), core))
    for f in both:
        inner_start(f, 0)
    for f in both:
        outer_send(f, 0, 0)
    for f in both:
        inner_forward(f, 0)
    for f in both:
        inner_rest(f, 0)
    for f in both:
        inner_finish(f, 0)
        b_start(f, 0, 0)
        b_local(f, 0, 0, 0)
        b_start(f, 0, 1)
        b_local(f, 0, 0, 1)
        b_start(f, 0, 2)
        b_local(f, 0, 0, 2)
        b_start(f, 0, 3)
        b_local(f, 0, 0, 3)
    for f in both:
        outer_forward(f, 0, 0)
    for f in both:
        outer_rest(f, 0, 0)
        b_start(f, 1, 0)
        b_local(f, 0, 1, 0)
        b_start(f, 2, 0)
        b_local(f, 0, 2, 0)
    for f in both:
        outer_forward(f, 0, 1)
    for f in both:
        outer_rest(f, 0, 1)
        b_start(f, 1, 1)
        b_local(f, 0, 1, 1)
        b_start(f, 2, 1)
        b_local(f, 0, 2, 1)
    for f in both:
        arrived(slot(f, 1, 0, 0), z_recv.at[f])
        inner_start(f, 1)
        outer_send(f, 1, 0)
    for f in both:
        outer_forward(f, 0, 2)
    for f in both:
        outer_rest(f, 0, 2)
        b_start(f, 1, 2)
        b_local(f, 0, 1, 2)
        b_start(f, 2, 2)
        b_local(f, 0, 2, 2)
    for f in both:
        outer_forward(f, 0, 3)
    for f in both:
        outer_rest(f, 0, 3)
        b_start(f, 1, 3)
        b_local(f, 0, 1, 3)
        b_start(f, 2, 3)
        b_local(f, 0, 2, 3)
    b_nearest(0)
    for f in both:
        inner_forward(f, 1)
    for f in both:
        inner_rest(f, 1)
    for f in both:
        outer_finish(f, 0, 0)
        b_start(f, 3, 0)
        b_local(f, 0, 3, 0)
    for f in both:
        outer_finish(f, 0, 1)
        b_start(f, 3, 1)
        b_local(f, 0, 3, 1)
    for f in both:
        outer_finish(f, 0, 2)
        b_start(f, 3, 2)
        b_local(f, 0, 3, 2)
    for f in both:
        outer_finish(f, 0, 3)
        b_start(f, 3, 3)
        b_local(f, 0, 3, 3)
    for f in both:
        inner_finish(f, 1)
    for f in both:
        b_local(f, 1, 0, 0)
        b_local(f, 1, 0, 1)
        b_local(f, 1, 0, 2)
        b_local(f, 1, 0, 3)
    for f in both:
        outer_forward(f, 1, 0)
    for f in both:
        outer_forward(f, 1, 1)
    b_rest(0)
    for f in both:
        outer_rest(f, 1, 0)
        b_local(f, 1, 1, 0)
        b_local(f, 1, 2, 0)
    b_nearest(1)
    b_nearest(2)
    for f in both:
        outer_forward(f, 1, 2)
    work(0, 0, first=True)
    work(1, 0)
    for f in both:
        outer_rest(f, 1, 1)
        b_local(f, 1, 1, 1)
        b_local(f, 1, 2, 1)
    b_rest(1)
    b_rest(2)
    b_nearest(3)
    work(0, 1)
    for f in both:
        outer_forward(f, 1, 3)
    work(0, 2)
    for f in both:
        outer_rest(f, 1, 2)
        b_local(f, 1, 1, 2)
        b_local(f, 1, 2, 2)
    for f in both:
        outer_rest(f, 1, 3)
        b_local(f, 1, 1, 3)
        b_local(f, 1, 2, 3)
    b_rest(3)
    work(0, 3)
    work(1, 1)
    work(1, 2)
    for f in both:
        outer_finish(f, 1, 0)
        b_local(f, 1, 3, 0)
    for f in both:
        outer_finish(f, 1, 1)
        b_local(f, 1, 3, 1)
    for f in both:
        outer_finish(f, 1, 2)
        b_local(f, 1, 3, 2)
    for f in both:
        outer_finish(f, 1, 3)
        b_local(f, 1, 3, 3)
    work(1, 3, last=True)

    def drain(ref, send_sem, when=None):
        wait = pltpu.make_async_remote_copy(
            src_ref=ref,
            dst_ref=ref,
            send_sem=send_sem,
            recv_sem=z_recv.at[0],
            device_id=sibling,
            device_id_type=MESH,
        ).wait_send
        if when is None:
            wait()
        else:
            pl.when(when)(wait)

    drain(gathered.at[0, 0, pl.ds(0, 2)], a_send.at[0])
    drain(gathered.at[0, 0, 0], a_send.at[1])
    drain(gathered.at[0], a_send.at[2])
    drain(gathered.at[0, 0], a_send.at[3])
    drain(gathered.at[0, 0, 0, pl.ds(0, 2)], a_send.at[4])
    drain(partner, b_side.at[0], owner)
    for k, n, _, when in b_targets():
        drain(partner.at[0], b_send.at[k, n], when)
    for r in both:
        for f in both:
            for nearest in (True, False):
                mine, goes_on, _ = b_mine(f, r, nearest)
                drain(partner.at[0, 0], b_far.at[int(nearest), r, f], mine)
                if nearest:
                    drain(partner.at[0, 0], b_pass.at[r, f], goes_on)


def whiten(spectra, valid):
    kept = valid.astype(jnp.float32)
    white = []
    for f in range(2):
        real = spectra[2 * f].astype(jnp.float32)
        imag = spectra[2 * f + 1].astype(jnp.float32)
        factor = kept / jnp.maximum(jnp.sqrt(real * real + imag * imag), 0.5)
        white += [(real * factor).astype(jnp.bfloat16), (imag * factor).astype(jnp.bfloat16)]
    return white


def on_device(spectra, valid):
    planes, windows, rows = spectra.shape
    width = rows // 4
    total = windows * lax.axis_size("col")
    norm = 1.0 / float(total) ** 0.5
    dma = pltpu.SemaphoreType.DMA
    vmem = pl.BlockSpec(memory_space=pltpu.VMEM)
    return pl.pallas_call(
        functools.partial(kernel, norm),
        out_shape=jax.ShapeDtypeStruct((2, planes // 2, rows, width), jnp.float32),
        in_specs=[vmem] * 4,
        out_specs=vmem,
        scratch_shapes=[
            pltpu.VMEM((2, 2, RING, RING, 2, windows, rows), jnp.bfloat16),
            pltpu.VMEM((2, 2, RING, RING, 2, windows, width), jnp.bfloat16),
            dma((5,)),
            dma((2,)),
            dma((2, 2, 2, 2)),
            dma((2, 2)),
            dma((2, 2, 2, 4)),
            dma((2, 2, 4)),
            dma((2, 2, 4)),
            dma((2, 2)),
            dma((2, 2)),
            dma((2, 2, 2)),
            dma((1,)),
            dma((2, 2, 4)),
        ],
        compiler_params=pltpu.CompilerParams(
            collective_id=0, has_side_effects=True, vmem_limit_bytes=48 * 2**20
        ),
        cost_estimate=pl.CostEstimate(
            flops=16 * total * rows * width, bytes_accessed=2**22, transcendentals=0
        ),
    )(*whiten(spectra, valid))


def solution(mesh):
    placed = (P(None, "col", "row"), P("col", "row"))
    return jax.shard_map(
        on_device,
        mesh=mesh,
        in_specs=placed,
        out_specs=P(None, None, "row", "col"),
        check_vma=False,
    )
```
